128 devices in a mesh: seq: 128 (over y, x, z, core).
Axes of the slice: x: 4, y: 4, z: 4, core: 2. Of those that a mesh axis runs over, the one named last changes fastest.
Arguments:
- queries: bfloat16 [524288, 768], P('seq'), may hold values from -8 to 8
- key_rows: bfloat16 [524288, 768], P('seq'), may hold values from -8 to 8
- value_rows: bfloat16 [524288, 768], P('seq'), may hold values from -6 to 6
Outputs:
- mixed: bfloat16 [524288, 768], P('seq')
The draws below stay inside these ranges and needn't reach their ends.
All inputs are finite; a program needn't handle non-finite values.
Results may differ from the reference program's by a relative error of at most 0.0037.
Values may be sent and summed in bfloat16 or wider, within the bound.
No kernel may reach another device: no remote copies, remote signals or barrier semaphores. Data moves between devices by JAX's collectives and lax.ppermute only.
A program may use at most 128 MiB of HBM per device.

```python
import jax
import jax.numpy as jnp
from jax import lax

D = 768
HEADS = 12
BLOCK = 512
KEEP = 512
TOKENS = 524288


def draw_queries(key, part):
    key = jax.random.fold_in(key, 1)
    values = jnp.clip(jax.random.normal(key, (TOKENS, D), jnp.float32), -6.0, 6.0)
    return values.astype(jnp.bfloat16)


def draw_key_rows(key, part):
    key = jax.random.fold_in(key, 2)
    values = jnp.clip(jax.random.normal(key, (TOKENS, D), jnp.float32), -6.0, 6.0)
    return values.astype(jnp.bfloat16)


def level_of(rng, extent, cuts, least, largest):
    factor_of = 1.0
    for dim, shards_of in cuts:
        heights = jax.random.uniform(jax.random.fold_in(jax.random.fold_in(rng, 6), dim), (shards_of,), jnp.float32, least / len(cuts), largest / len(cuts))
        factor_of = factor_of * jnp.repeat(jnp.exp(heights), extent[dim] // shards_of).reshape((-1,) + (1,) * (len(extent) - 1 - dim))
    return factor_of


def noise(rng, dims, spread, most, cuts=(), kind=jnp.bfloat16):
    values = jax.random.normal(rng, dims, jnp.float32) * spread
    if len(cuts) > 0:
        values = level_of(rng, dims, cuts, -0.22, 0.18) * values
    return jnp.clip(values, min=-most, max=most).astype(kind)


def setup_inputs(seed: int = 0) -> dict:
    key_list = jax.random.split(jax.random.key(seed), 4)
    queries = draw_queries(jax.random.fold_in(key_list[3], 71), 0)
    key_rows = draw_key_rows(jax.random.fold_in(key_list[3], 71), 0)
    value_rows = noise(key_list[2], (TOKENS, D), 1.0, 6.0, ((0, 128),))
    return {"queries": queries, "key_rows": key_rows, "value_rows": value_rows}


masked_score = -1e30


def pick(array, stride):
    head_count = array.shape[1]
    shaped = array.reshape((array.shape[0] // stride, stride) + array.shape[1:])[:, :head_count]
    return jnp.moveaxis(jnp.diagonal(shaped, axis1=1, axis2=2), -1, 1)


def put_back(complete, merged, stride):
    total_rows, head_count, head_size = complete.shape
    shaped = complete.reshape(total_rows // stride, stride, head_count, head_size)
    diagonal_mask = jnp.eye(head_count, dtype=bool)
    corner = jnp.where(diagonal_mask[None, :, :, None], merged[:, None, :, :], shaped[:, :head_count])
    shaped = jnp.concatenate([corner, shaped[:, head_count:]], 1)
    return shaped.reshape(complete.shape)


def attend(query_set, key_set, value_set, query_place, key_place):
    factor = query_set.shape[-1] ** -0.5
    scores = jnp.einsum("qhe,khe->hqk", query_set.astype(jnp.float32), key_set.astype(jnp.float32), precision=lax.Precision.HIGHEST) * factor
    scores = jnp.where(key_place[None, None, :] <= query_place[None, :, None], scores, masked_score)
    highest = jnp.max(scores, axis=-1)
    expanded = jnp.exp(scores - highest[..., None])
    totals = jnp.sum(expanded, axis=-1)
    probs = lax.optimization_barrier(expanded.astype(jnp.bfloat16))
    result = jnp.einsum("hqk,khe->qhe", probs.astype(jnp.float32), value_set.astype(jnp.float32), precision=lax.Precision.HIGHEST)
    result = result / jnp.transpose(totals)[..., None]
    return result, jnp.transpose(highest + jnp.log(totals))


def combine(out_zero, lse_zero, out_one, lse_one, out_two, lse_two, out_three, lse_three):
    row_ids = jnp.arange(out_zero.shape[0], dtype=jnp.int32)
    inside_two = (row_ids % 2 == 0)[:, None]
    inside_three = (row_ids % 4 == 0)[:, None]
    highest = jnp.maximum(lse_zero, lse_one)
    highest = jnp.where(inside_two, jnp.maximum(highest, lse_two), highest)
    highest = jnp.where(inside_three, jnp.maximum(highest, lse_three), highest)
    weight_zero = jnp.exp(lse_zero - highest)
    weight_one = jnp.exp(lse_one - highest)
    weight_two = jnp.where(inside_two, jnp.exp(lse_two - highest), 0.0)
    weight_three = jnp.where(inside_three, jnp.exp(lse_three - highest), 0.0)
    summed = weight_zero[..., None] * out_zero + weight_one[..., None] * out_one
    summed = summed + weight_two[..., None] * out_two + weight_three[..., None] * out_three
    return summed / (weight_zero + weight_one + weight_two + weight_three)[..., None]


def reference(queries, key_rows, value_rows):
    tokens, model_width = queries.shape
    head_count = HEADS
    head_size = model_width // head_count
    query_heads = queries.reshape(tokens, head_count, head_size)
    key_heads = key_rows.reshape(tokens, head_count, head_size)
    value_heads = value_rows.reshape(tokens, head_count, head_size)
    blocks = tokens // BLOCK
    places = jnp.arange(BLOCK, dtype=jnp.int32)

    def local_block(triple):
        return attend(triple[0], triple[1], triple[2], places, places)

    shape_blocks = (blocks, BLOCK, head_count, head_size)
    out_zero, lse_zero = lax.map(local_block, (query_heads.reshape(shape_blocks), key_heads.reshape(shape_blocks), value_heads.reshape(shape_blocks)))
    out_zero = out_zero.reshape(tokens, head_count, head_size)
    lse_zero = lse_zero.reshape(tokens, head_count)
    stride = tokens // (4 * KEEP)
    query_one = pick(query_heads, stride)
    key_one = pick(key_heads, stride)
    value_one = pick(value_heads, stride)
    keep_places = jnp.arange(KEEP, dtype=jnp.int32)

    def segment_attend(query_set, key_set, value_set):
        return attend(query_set, key_set, value_set, keep_places, keep_places)

    def level(segment_count, query_set, key_set, value_set):
        shape_level = (segment_count, KEEP, head_count, head_size)
        result, lse_level = jax.vmap(segment_attend)(query_set.reshape(shape_level), key_set.reshape(shape_level), value_set.reshape(shape_level))
        return result.reshape(segment_count * KEEP, head_count, head_size), lse_level.reshape(segment_count * KEEP, head_count)

    out_one, lse_one = level(4, query_one, key_one, value_one)
    out_two, lse_two = level(2, query_one[::2], key_one[::2], value_one[::2])
    out_three, lse_three = level(1, query_one[::4], key_one[::4], value_one[::4])
    merged = combine(pick(out_zero, stride), pick(lse_zero, stride), out_one, lse_one,
                     jnp.repeat(out_two, 2, axis=0), jnp.repeat(lse_two, 2, axis=0),
                     jnp.repeat(out_three, 4, axis=0), jnp.repeat(lse_three, 4, axis=0))
    return put_back(out_zero, merged, stride).astype(jnp.bfloat16).reshape(tokens, model_width)
```

```python
import jax
import jax.numpy as jnp
from jax import lax
from jax.experimental import pallas as pl
from jax.experimental.pallas import tpu as pltpu
from jax.sharding import PartitionSpec as P

HEADS = 12
HEAD = 64
PAIR = 2 * HEAD
BLOCK = 512
HALF = BLOCK // 2
WIDTH = HEADS * HEAD
ROWS = 16
STRIDE = 256
UNIT = 2 * ROWS
VMEM = 52 << 20

MASKED = -1e30
BF16 = jnp.bfloat16
F32 = jnp.float32
TRANSPOSED = (((1,), (1,)), ((), ()))

CHUNKS = (1, 2, 4, 1)


def owner_mask(rows, row_size, columns):
    row = lax.broadcasted_iota(jnp.int32, (rows, columns), 0) // row_size
    head = lax.broadcasted_iota(jnp.int32, (rows, columns), 1) // HEAD
    return row == head


def pick_kernel(q_ref, k_ref, v_ref, q_out, kv_out):
    owned = owner_mask(ROWS, 1, WIDTH)
    for ref, out, start in ((q_ref, q_out, 0), (k_ref, kv_out, 0), (v_ref, kv_out, WIDTH)):
        rows = [
            jnp.sum(jnp.where(owned, ref[i].astype(F32), 0.0), axis=0, keepdims=True)
            for i in range(ROWS)
        ]
        out[:, start : start + WIDTH] = jnp.concatenate(rows, 0).astype(BF16)


def pick(queries, key_rows, value_rows):
    spec = pl.BlockSpec((ROWS, ROWS, WIDTH), lambda i: (0, 0, 0))
    shape = (ROWS, STRIDE, WIDTH)
    return pl.pallas_call(
        pick_kernel,
        grid=(1,),
        in_specs=[spec] * 3,
        out_specs=[
            pl.BlockSpec((ROWS, WIDTH), lambda i: (0, 0)),
            pl.BlockSpec((ROWS, 2 * WIDTH), lambda i: (0, 0)),
        ],
        out_shape=[
            jax.ShapeDtypeStruct((ROWS, WIDTH), BF16),
            jax.ShapeDtypeStruct((ROWS, 2 * WIDTH), BF16),
        ],
        compiler_params=pltpu.CompilerParams(vmem_limit_bytes=VMEM),
        name="pick",
    )(queries.reshape(shape), key_rows.reshape(shape), value_rows.reshape(shape))


def select_kernel(own_ref, one_ref, two_ref, three_ref, out_ref):
    row = lax.broadcasted_iota(jnp.int32, (UNIT, 4 * ROWS), 0)
    column = lax.broadcasted_iota(jnp.int32, (UNIT, 4 * ROWS), 1)
    source = jnp.where(
        row < 16,
        row,
        jnp.where(
            row < 24,
            16 + 2 * (row - 16),
            jnp.where(row < 28, 32 + 4 * (row - 24), 48 + 4 * (row - 28)),
        ),
    )
    chosen = (column == source).astype(BF16)
    every = jnp.concatenate([own_ref[...], one_ref[...], two_ref[...], three_ref[...]], 0)
    out_ref[...] = jnp.dot(chosen, every, preferred_element_type=F32).astype(BF16)


def select(own, one, two, three):
    return pl.pallas_call(
        select_kernel,
        out_shape=jax.ShapeDtypeStruct((UNIT, 2 * WIDTH), BF16),
        name="select",
    )(own, one, two, three)


def local_kernel(q_ref, k_ref, v_ref, *refs):
    out_ref, kept_ref = refs[-2:]
    low = lax.broadcasted_iota(jnp.int32, (1, PAIR), 1) < HEAD
    keep = lax.broadcasted_iota(jnp.int32, (HALF, HALF), 1) <= lax.broadcasted_iota(
        jnp.int32, (HALF, HALF), 0
    )

    def columns(pair):
        return slice(pair * PAIR, (pair + 1) * PAIR)

    def scores(pair):
        query = q_ref[:, columns(pair)] * jnp.asarray(HEAD**-0.5, BF16)
        key = k_ref[:, columns(pair)]
        zero = jnp.zeros_like(query)
        even, odd = jnp.where(low, query, zero), jnp.where(low, zero, query)
        early = lax.dot_general(
            jnp.concatenate([even, odd], 0), key[:HALF], TRANSPOSED, preferred_element_type=F32
        )
        late = lax.dot_general(
            jnp.concatenate([even[HALF:], odd[HALF:]], 0),
            key[HALF:],
            TRANSPOSED,
            preferred_element_type=F32,
        )
        return ((early[:BLOCK], late[:HALF]), (early[BLOCK:], late[HALF:]))

    def soften(pieces):
        results = []
        for early, late in pieces:
            first_half = jnp.where(keep, early[:HALF], MASKED)
            before = early[HALF:]
            second_half = jnp.where(keep, late, MASKED)
            top_one = jnp.max(first_half, axis=1, keepdims=True)
            top_two = jnp.max(jnp.maximum(before, second_half), axis=1, keepdims=True)
            results.append(
                (
                    jnp.exp(first_half - top_one).astype(BF16),
                    jnp.exp(before - top_two).astype(BF16),
                    jnp.exp(second_half - top_two).astype(BF16),
                    top_one,
                    top_two,
                )
            )
        return results

    def finish(pair, probs):
        value = v_ref[:, columns(pair)]
        extended = jnp.concatenate([value, jnp.ones_like(value)], 1)
        even, odd = probs
        one = jnp.dot(
            jnp.concatenate([even[0], odd[0]], 0), extended[:HALF], preferred_element_type=F32
        )
        two = jnp.dot(
            jnp.concatenate(
                [
                    jnp.concatenate([even[1], odd[1]], 0),
                    jnp.concatenate([even[2], odd[2]], 0),
                ],
                1,
            ),
            extended,
            preferred_element_type=F32,
        )
        for half, both in enumerate((one, two)):
            upper = jnp.where(low, both[:HALF, :PAIR], both[HALF:, :PAIR])
            lower = jnp.where(low, both[:HALF, PAIR:], both[HALF:, PAIR:])
            out_ref[half * HALF : (half + 1) * HALF, columns(pair)] = (upper / lower).astype(BF16)
            a, b = 2 * pair, 2 * pair + 1
            top_a = jnp.broadcast_to(even[3 + half][a : a + 1], (1, PAIR))
            top_b = jnp.broadcast_to(odd[3 + half][b : b + 1], (1, PAIR))
            for start, row in (
                (0, jnp.where(low, upper[a : a + 1], upper[b : b + 1])),
                (2, jnp.where(low, lower[a : a + 1], lower[b : b + 1])),
                (4, jnp.where(low, top_a, top_b)),
            ):
                kept_ref[start + half : start + half + 1, columns(pair)] = row

    ready = scores(0)
    for pair in range(HEADS // 2):
        later = scores(pair + 1) if pair + 1 < HEADS // 2 else None
        finish(pair, soften(ready))
        ready = later


def local_level(first, count, arrays, complete):
    spec = pl.BlockSpec((BLOCK, WIDTH), lambda i: (first + i, 0))
    operands = list(arrays)
    in_specs = [spec] * 3
    aliases = {}
    if complete is not None:
        operands.append(complete)
        in_specs.append(pl.BlockSpec(memory_space=pl.ANY))
        aliases = {3: 0}
    return pl.pallas_call(
        local_kernel,
        grid=(count,),
        in_specs=in_specs,
        out_specs=[spec, pl.BlockSpec((8, WIDTH), lambda i: (i, 0))],
        out_shape=[
            jax.ShapeDtypeStruct(arrays[0].shape, BF16),
            jax.ShapeDtypeStruct((8 * count, WIDTH), F32),
        ],
        input_output_aliases=aliases,
        compiler_params=pltpu.CompilerParams(vmem_limit_bytes=VMEM),
        cost_estimate=pl.CostEstimate(
            flops=count * HEADS * 4 * BLOCK * BLOCK * HEAD * 4,
            bytes_accessed=count * 8 * BLOCK * WIDTH,
            transcendentals=count * HEADS * BLOCK * BLOCK,
        ),
        name="local",
    )(*operands)


def merge_kernel(spot_ref, q_ref, own_ref, other_ref, *refs):
    kept_refs, old_ref, out_ref = refs[:-2], refs[-2], refs[-1]
    lanes = HEADS * ROWS
    owned = owner_mask(lanes, ROWS, WIDTH)
    query = q_ref[...] * jnp.asarray(HEAD**-0.5, BF16)
    spread = jnp.where(owned, jnp.concatenate([query] * HEADS, 0), jnp.zeros((), BF16))
    score = jnp.concatenate(
        [
            lax.dot_general(spread, ref[:, :WIDTH], TRANSPOSED, preferred_element_type=F32)
            for ref in (own_ref, other_ref)
        ],
        1,
    )
    keys = score.shape[1]
    device = spot_ref[0]
    column = lax.broadcasted_iota(jnp.int32, (1, keys), 1)
    core, x, z = column // (keys // 2), column // (4 * UNIT) % 4, column // UNIT % 4
    inner = column % UNIT
    quarter = jnp.where(inner < 16, 0, jnp.where(inner < 24, 1, jnp.where(inner < 28, 2, 3)))
    index = jnp.where(
        inner < 16, inner, jnp.where(inner < 24, 2 * (inner - 16), 4 * (inner % 4))
    )
    source = jnp.bitwise_xor(device, quarter * 32 + x * 8 + z * 2 + core)
    key_place = source * ROWS + index
    row = lax.broadcasted_iota(jnp.int32, (lanes, 1), 0) % ROWS
    query_place = device * ROWS + row
    in_one = (quarter == 0).astype(F32)
    in_two = jnp.where((quarter <= 1) & (index % 2 == 0), 1.0, 0.0)
    in_three = jnp.where(index % 4 == 0, 1.0, 0.0)
    has_two = jnp.where(row % 2 == 0, 1.0, 0.0)
    has_three = jnp.where(row % 4 == 0, 1.0, 0.0)
    count = in_one + has_two * in_two + has_three * in_three
    count = jnp.where(key_place <= query_place, count, 0.0)
    score = jnp.where(count > 0.0, score, MASKED)
    top = jnp.max(score, axis=1, keepdims=True)
    probs = jnp.exp(score - top) * count
    total = jnp.sum(probs, axis=1, keepdims=True)
    probs = probs.astype(BF16)
    result = jnp.dot(probs[:, : keys // 2], own_ref[:, WIDTH:], preferred_element_type=F32)
    result = result + jnp.dot(
        probs[:, keys // 2 :], other_ref[:, WIDTH:], preferred_element_type=F32
    )

    def gather_heads(array):
        kept = jnp.where(owned, array, 0.0)
        return jnp.sum(kept.reshape(HEADS, ROWS, WIDTH), axis=0)

    top, total, result = gather_heads(top), gather_heads(total), gather_heads(result)
    blocks = [ref[8 * i : 8 * i + 8] for ref in kept_refs for i in range(ref.shape[0] // 8)]
    result_zero, total_zero, top_zero = (
        jnp.concatenate([block[start : start + 2] for block in blocks], 0) for start in (0, 2, 4)
    )
    best = jnp.maximum(top, top_zero)
    weight, weight_zero = jnp.exp(top - best), jnp.exp(top_zero - best)
    mixed = (weight * result + weight_zero * result_zero) / (
        weight * total + weight_zero * total_zero
    )
    owned = owner_mask(ROWS, 1, WIDTH)
    for i in range(ROWS):
        out_ref[i] = jnp.where(owned, mixed[i : i + 1], old_ref[i].astype(F32)).astype(BF16)


def merge(spot, query, own, other, kept, complete):
    shape = (ROWS, STRIDE, WIDTH)
    corner = pl.BlockSpec((ROWS, ROWS, WIDTH), lambda i: (0, 0, 0))

    def whole(array):
        return pl.BlockSpec(array.shape, lambda i: (0, 0))

    merged = pl.pallas_call(
        merge_kernel,
        grid=(1,),
        in_specs=[pl.BlockSpec(memory_space=pltpu.SMEM)]
        + [whole(array) for array in (query, own, other, *kept)]
        + [corner],
        out_specs=corner,
        out_shape=jax.ShapeDtypeStruct(shape, BF16),
        input_output_aliases={4 + len(kept): 0},
        compiler_params=pltpu.CompilerParams(vmem_limit_bytes=VMEM),
        name="merge",
    )(spot, query, own, other, *kept, complete.reshape(shape))
    return merged.reshape(complete.shape)


def local(queries, key_rows, value_rows):
    devices = lax.axis_size("seq")
    arrays = (queries, key_rows, value_rows)

    def exchange(array, distance):
        return lax.ppermute(array, "seq", [(i, i ^ distance) for i in range(devices)])

    query, rows = pick(*arrays)
    complete, kept, first = None, [], 0
    stages = ((32, 64, 96), (2, 4, 6), (8, 16, 24), (1,))
    for stage, (distances, count) in enumerate(zip(stages, CHUNKS)):
        received = [exchange(rows, distance) for distance in distances]
        complete, some = local_level(first, count, arrays, complete)
        first += count
        kept.append(some)
        received, rows, complete = lax.optimization_barrier((received, rows, complete))
        if stage == 0:
            rows = select(rows, *received)
        elif stage < 3:
            rows = jnp.concatenate([rows, *received], 0)
        if stage < 3:
            rows, complete, arrays = lax.optimization_barrier((rows, complete, arrays))
    spot = lax.axis_index("seq").astype(jnp.int32).reshape(1)
    return merge(spot, query, rows, received[0], kept, complete)


def solution(mesh):
    in_specs = (P("seq", None), P("seq", None), P("seq", None))
    out_specs = P("seq", None)
    return jax.shard_map(local, mesh=mesh, in_specs=in_specs, out_specs=out_specs, check_vma=False)
```

```python
import jax
import jax.numpy as jnp
from jax import lax
from jax.experimental import pallas as pl
from jax.experimental.pallas import tpu as pltpu
from jax.sharding import PartitionSpec as P

HEADS = 12
HEAD = 64
PAIR = 2 * HEAD
BLOCK = 512
HALF = BLOCK // 2
WIDTH = HEADS * HEAD
ROWS = 16
STRIDE = 256
UNIT = 2 * ROWS
VMEM = 52 << 20
LOCAL_VMEM = 52 << 20
MERGE_VMEM = 20 << 20

MASKED = -1e30
BF16 = jnp.bfloat16
F32 = jnp.float32
TRANSPOSED = (((1,), (1,)), ((), ()))

CHUNKS = (1, 2, 4, 1)


def owner_mask(rows, row_size, columns):
    row = lax.broadcasted_iota(jnp.int32, (rows, columns), 0) // row_size
    head = lax.broadcasted_iota(jnp.int32, (rows, columns), 1) // HEAD
    return row == head


def pick_kernel(q_ref, k_ref, v_ref, q_out, own_out, second_out, low_out, high_out):
    owned = owner_mask(ROWS, 1, WIDTH)

    def diagonal(ref):
        return [
            jnp.sum(jnp.where(owned, ref[i].astype(F32), 0.0), axis=0, keepdims=True)
            for i in range(ROWS)
        ]

    def pack(rows):
        return jnp.concatenate(rows, 0).astype(BF16)

    q_out[...] = pack(diagonal(q_ref))
    for ref, columns in ((k_ref, slice(0, WIDTH)), (v_ref, slice(WIDTH, 2 * WIDTH))):
        rows = diagonal(ref)
        none = [jnp.zeros_like(rows[0])] * (ROWS // 4)
        own_out[:, columns] = pack(rows)
        second_out[:, columns] = pack(rows[::2])
        low_out[:, columns] = pack(rows[::4] + none)
        high_out[:, columns] = pack(none + rows[::4])


def pick(queries, key_rows, value_rows):
    spec = pl.BlockSpec((ROWS, ROWS, WIDTH), lambda i: (0, 0, 0))
    shape = (ROWS, STRIDE, WIDTH)
    outs = [
        jax.ShapeDtypeStruct(size, BF16)
        for size in ((ROWS, WIDTH), (ROWS, 2 * WIDTH)) + ((ROWS // 2, 2 * WIDTH),) * 3
    ]
    return pl.pallas_call(
        pick_kernel,
        grid=(1,),
        in_specs=[spec] * 3,
        out_specs=[pl.BlockSpec(out.shape, lambda i: (0, 0)) for out in outs],
        out_shape=outs,
        compiler_params=pltpu.CompilerParams(vmem_limit_bytes=VMEM),
        name="pick",
    )(queries.reshape(shape), key_rows.reshape(shape), value_rows.reshape(shape))


def local_kernel(q_ref, k_ref, v_ref, *refs):
    out_ref, kept_ref = refs[-2:]
    low = lax.broadcasted_iota(jnp.int32, (1, PAIR), 1) < HEAD
    keep = lax.broadcasted_iota(jnp.int32, (HALF, HALF), 1) <= lax.broadcasted_iota(
        jnp.int32, (HALF, HALF), 0
    )

    def columns(pair):
        return slice(pair * PAIR, (pair + 1) * PAIR)

    def scores(pair):
        query = q_ref[:, columns(pair)] * jnp.asarray(HEAD**-0.5, BF16)
        key = k_ref[:, columns(pair)]
        zero = jnp.zeros_like(query)
        even, odd = jnp.where(low, query, zero), jnp.where(low, zero, query)
        early = lax.dot_general(
            jnp.concatenate([even, odd], 0), key[:HALF], TRANSPOSED, preferred_element_type=F32
        )
        late = lax.dot_general(
            jnp.concatenate([even[HALF:], odd[HALF:]], 0),
            key[HALF:],
            TRANSPOSED,
            preferred_element_type=F32,
        )
        return ((early[:BLOCK], late[:HALF]), (early[BLOCK:], late[HALF:]))

    def soften(pieces):
        results = []
        for early, late in pieces:
            first_half = jnp.where(keep, early[:HALF], MASKED)
            before = early[HALF:]
            second_half = jnp.where(keep, late, MASKED)
            top_one = jnp.max(first_half, axis=1, keepdims=True)
            top_two = jnp.max(jnp.maximum(before, second_half), axis=1, keepdims=True)
            results.append(
                (
                    jnp.exp(first_half - top_one).astype(BF16),
                    jnp.exp(before - top_two).astype(BF16),
                    jnp.exp(second_half - top_two).astype(BF16),
                    top_one,
                    top_two,
                )
            )
        return results

    def finish(pair, probs):
        value = v_ref[:, columns(pair)]
        extended = jnp.concatenate([value, jnp.ones_like(value)], 1)
        even, odd = probs
        one = jnp.dot(
            jnp.concatenate([even[0], odd[0]], 0), extended[:HALF], preferred_element_type=F32
        )
        two = jnp.dot(
            jnp.concatenate(
                [
                    jnp.concatenate([even[1], odd[1]], 0),
                    jnp.concatenate([even[2], odd[2]], 0),
                ],
                1,
            ),
            extended,
            preferred_element_type=F32,
        )
        for half, both in enumerate((one, two)):
            upper = jnp.where(low, both[:HALF, :PAIR], both[HALF:, :PAIR])
            lower = jnp.where(low, both[:HALF, PAIR:], both[HALF:, PAIR:])
            out_ref[half * HALF : (half + 1) * HALF, columns(pair)] = (upper / lower).astype(BF16)
            a, b = 2 * pair, 2 * pair + 1
            top_a = jnp.broadcast_to(even[3 + half][a : a + 1], (1, PAIR))
            top_b = jnp.broadcast_to(odd[3 + half][b : b + 1], (1, PAIR))
            for start, row in (
                (0, jnp.where(low, upper[a : a + 1], upper[b : b + 1])),
                (2, jnp.where(low, lower[a : a + 1], lower[b : b + 1])),
                (4, jnp.where(low, top_a, top_b)),
            ):
                kept_ref[start + half : start + half + 1, columns(pair)] = row

    ready = scores(0)
    for pair in range(HEADS // 2):
        later = scores(pair + 1) if pair + 1 < HEADS // 2 else None
        finish(pair, soften(ready))
        ready = later


def local_level(first, count, arrays, complete):
    spec = pl.BlockSpec((BLOCK, WIDTH), lambda i: (first + i, 0))
    operands = list(arrays)
    in_specs = [spec] * 3
    aliases = {}
    if complete is not None:
        operands.append(complete)
        in_specs.append(pl.BlockSpec(memory_space=pl.ANY))
        aliases = {3: 0}
    return pl.pallas_call(
        local_kernel,
        grid=(count,),
        in_specs=in_specs,
        out_specs=[spec, pl.BlockSpec((8, WIDTH), lambda i: (i, 0))],
        out_shape=[
            jax.ShapeDtypeStruct(arrays[0].shape, BF16),
            jax.ShapeDtypeStruct((8 * count, WIDTH), F32),
        ],
        input_output_aliases=aliases,
        compiler_params=pltpu.CompilerParams(vmem_limit_bytes=LOCAL_VMEM),
        cost_estimate=pl.CostEstimate(
            flops=count * HEADS * 4 * BLOCK * BLOCK * HEAD * 4,
            bytes_accessed=count * 8 * BLOCK * WIDTH,
            transcendentals=count * HEADS * BLOCK * BLOCK,
        ),
        name="local",
    )(*operands)


def merge_kernel(spot_ref, q_ref, own_ref, other_ref, *refs):
    kept_refs, old_ref, out_ref = refs[:-2], refs[-2], refs[-1]
    lanes = HEADS * ROWS
    owned = owner_mask(lanes, ROWS, WIDTH)
    query = q_ref[...] * jnp.asarray(HEAD**-0.5, BF16)
    spread = jnp.where(owned, jnp.concatenate([query] * HEADS, 0), jnp.zeros((), BF16))
    score = jnp.concatenate(
        [
            lax.dot_general(spread, ref[:, :WIDTH], TRANSPOSED, preferred_element_type=F32)
            for ref in (own_ref, other_ref)
        ],
        1,
    )
    keys = score.shape[1]
    device = spot_ref[0]
    column = lax.broadcasted_iota(jnp.int32, (1, keys), 1)
    core, x, z = column // (keys // 2), column // (4 * UNIT) % 4, column // UNIT % 4
    inner = column % UNIT
    quarter = jnp.where(inner < 16, 0, jnp.where(inner < 24, 1, jnp.where(inner < 28, 2, 3)))
    index = jnp.where(
        inner < 16, inner, jnp.where(inner < 24, 2 * (inner - 16), 4 * (inner % 4))
    )
    source = jnp.bitwise_xor(device, quarter * 32 + x * 8 + z * 2 + core)
    key_place = source * ROWS + index
    row = lax.broadcasted_iota(jnp.int32, (lanes, 1), 0) % ROWS
    query_place = device * ROWS + row
    in_one = (quarter == 0).astype(F32)
    in_two = jnp.where((quarter <= 1) & (index % 2 == 0), 1.0, 0.0)
    in_three = jnp.where(index % 4 == 0, 1.0, 0.0)
    has_two = jnp.where(row % 2 == 0, 1.0, 0.0)
    has_three = jnp.where(row % 4 == 0, 1.0, 0.0)
    count = in_one + has_two * in_two + has_three * in_three
    count = jnp.where(key_place <= query_place, count, 0.0)
    score = jnp.where(count > 0.0, score, MASKED)
    top = jnp.max(score, axis=1, keepdims=True)
    probs = jnp.exp(score - top) * count
    total = jnp.sum(probs, axis=1, keepdims=True)
    probs = probs.astype(BF16)
    result = jnp.dot(probs[:, : keys // 2], own_ref[:, WIDTH:], preferred_element_type=F32)
    result = result + jnp.dot(
        probs[:, keys // 2 :], other_ref[:, WIDTH:], preferred_element_type=F32
    )

    def gather_heads(array):
        kept = jnp.where(owned, array, 0.0)
        return jnp.sum(kept.reshape(HEADS, ROWS, WIDTH), axis=0)

    top, total, result = gather_heads(top), gather_heads(total), gather_heads(result)
    blocks = [ref[8 * i : 8 * i + 8] for ref in kept_refs for i in range(ref.shape[0] // 8)]
    result_zero, total_zero, top_zero = (
        jnp.concatenate([block[start : start + 2] for block in blocks], 0) for start in (0, 2, 4)
    )
    best = jnp.maximum(top, top_zero)
    weight, weight_zero = jnp.exp(top - best), jnp.exp(top_zero - best)
    mixed = (weight * result + weight_zero * result_zero) / (
        weight * total + weight_zero * total_zero
    )
    owned = owner_mask(ROWS, 1, WIDTH)
    for i in range(ROWS):
        out_ref[i] = jnp.where(owned, mixed[i : i + 1], old_ref[i].astype(F32)).astype(BF16)


def merge(spot, query, own, other, kept, complete):
    shape = (ROWS, STRIDE, WIDTH)
    corner = pl.BlockSpec((ROWS, ROWS, WIDTH), lambda i: (0, 0, 0))

    def whole(array):
        return pl.BlockSpec(array.shape, lambda i: (0, 0))

    merged = pl.pallas_call(
        merge_kernel,
        grid=(1,),
        in_specs=[pl.BlockSpec(memory_space=pltpu.SMEM)]
        + [whole(array) for array in (query, own, other, *kept)]
        + [corner],
        out_specs=corner,
        out_shape=jax.ShapeDtypeStruct(shape, BF16),
        input_output_aliases={4 + len(kept): 0},
        compiler_params=pltpu.CompilerParams(vmem_limit_bytes=MERGE_VMEM),
        name="merge",
    )(spot, query, own, other, *kept, complete.reshape(shape))
    return merged.reshape(complete.shape)


def local(queries, key_rows, value_rows):
    devices = lax.axis_size("seq")
    arrays = (queries, key_rows, value_rows)

    def exchange(array, distance):
        return lax.ppermute(array, "seq", [(i, i ^ distance) for i in range(devices)])

    query, rows, *sent = pick(*arrays)
    complete, kept, first = None, [], 0
    stages = ((32, 64, 96), (2, 4, 6), (8, 16, 24), (1,))
    for stage, (distances, count) in enumerate(zip(stages, CHUNKS)):
        if stage > 0:
            sent = [rows] * len(distances)
        received = [exchange(part, distance) for part, distance in zip(sent, distances)]
        complete, some = local_level(first, count, arrays, complete)
        first += count
        kept.append(some)
        received, rows, complete = lax.optimization_barrier((received, rows, complete))
        if stage == 0:
            rows = jnp.concatenate([rows, received[0], received[1] + received[2]], 0)
        elif stage < 3:
            rows = jnp.concatenate([rows, *received], 0)
        if stage < 3:
            rows, complete, arrays = lax.optimization_barrier((rows, complete, arrays))
    spot = lax.axis_index("seq").astype(jnp.int32).reshape(1)
    return merge(spot, query, rows, received[0], kept, complete)


def solution(mesh):
    in_specs = (P("seq", None), P("seq", None), P("seq", None))
    out_specs = P("seq", None)
    return jax.shard_map(local, mesh=mesh, in_specs=in_specs, out_specs=out_specs, check_vma=False)
```

```python
import jax
import jax.numpy as jnp
from jax import lax
from jax.experimental import pallas as pl
from jax.experimental.pallas import tpu as pltpu
from jax.sharding import PartitionSpec as P

HEADS = 12
HEAD = 64
PAIR = 2 * HEAD
BLOCK = 512
TILE = 128
TILES = BLOCK // TILE
PAIRS = HEADS // 2
WIDTH = HEADS * HEAD
ROWS = 16
STRIDE = 256
UNIT = 2 * ROWS
VMEM = 52 << 20
LOCAL_VMEM = 52 << 20
MERGE_VMEM = 20 << 20

MASKED = -1e30
BF16 = jnp.bfloat16
F32 = jnp.float32
TRANSPOSED = (((1,), (1,)), ((), ()))

CHUNKS = (0, 2, 5, 1)


def owner_mask(rows, row_size, columns):
    row = lax.broadcasted_iota(jnp.int32, (rows, columns), 0) // row_size
    head = lax.broadcasted_iota(jnp.int32, (rows, columns), 1) // HEAD
    return row == head


def pick_kernel(q_ref, k_ref, v_ref, q_out, own_out, second_out, low_out, high_out):
    owned = owner_mask(ROWS, 1, WIDTH)

    def diagonal(ref):
        return [
            jnp.sum(jnp.where(owned, ref[i].astype(F32), 0.0), axis=0, keepdims=True)
            for i in range(ROWS)
        ]

    def pack(rows):
        return jnp.concatenate(rows, 0).astype(BF16)

    q_out[...] = pack(diagonal(q_ref))
    for ref, columns in ((k_ref, slice(0, WIDTH)), (v_ref, slice(WIDTH, 2 * WIDTH))):
        rows = diagonal(ref)
        none = [jnp.zeros_like(rows[0])] * (ROWS // 4)
        own_out[:, columns] = pack(rows)
        second_out[:, columns] = pack(rows[::2])
        low_out[:, columns] = pack(rows[::4] + none)
        high_out[:, columns] = pack(none + rows[::4])


def pick(queries, key_rows, value_rows):
    spec = pl.BlockSpec((ROWS, ROWS, WIDTH), lambda i: (0, 0, 0))
    shape = (ROWS, STRIDE, WIDTH)
    outs = [
        jax.ShapeDtypeStruct(size, BF16)
        for size in ((ROWS, WIDTH), (ROWS, 2 * WIDTH)) + ((ROWS // 2, 2 * WIDTH),) * 3
    ]
    return pl.pallas_call(
        pick_kernel,
        grid=(1,),
        in_specs=[spec] * 3,
        out_specs=[pl.BlockSpec(out.shape, lambda i: (0, 0)) for out in outs],
        out_shape=outs,
        compiler_params=pltpu.CompilerParams(vmem_limit_bytes=VMEM),
        name="pick",
    )(queries.reshape(shape), key_rows.reshape(shape), value_rows.reshape(shape))


def local_kernel(q_ref, k_ref, v_ref, *refs):
    out_ref, kept_ref = refs[-2:]
    low = lax.broadcasted_iota(jnp.int32, (1, PAIR), 1) < HEAD
    keep = lax.broadcasted_iota(
        jnp.int32, (TILE, 2 * TILE), 1
    ) % TILE <= lax.broadcasted_iota(jnp.int32, (TILE, 2 * TILE), 0)
    zero = jnp.zeros((TILE, PAIR), BF16)
    one = jnp.ones((TILE, PAIR), BF16)
    counters = jnp.where(low, one, zero), jnp.where(low, zero, one)

    def columns(pair):
        return slice(pair * PAIR, (pair + 1) * PAIR)

    def score(pair, j):
        query = q_ref[j * TILE :, columns(pair)] * jnp.asarray(HEAD**-0.5, BF16)
        key = k_ref[j * TILE : (j + 1) * TILE, columns(pair)]
        both = jnp.concatenate([jnp.where(low, key, zero), jnp.where(low, zero, key)], 0)
        return lax.dot_general(query, both, TRANSPOSED, preferred_element_type=F32)

    def soften(scores, t):
        parts = [scores[j][(t - j) * TILE : (t - j + 1) * TILE] for j in range(t + 1)]
        parts[t] = jnp.where(keep, parts[t], MASKED)
        most = parts[0]
        for part in parts[1:]:
            most = jnp.maximum(most, part)
        tops = [
            jnp.broadcast_to(
                jnp.max(most[:, start : start + TILE], axis=1, keepdims=True), (TILE, TILE)
            )
            for start in (0, TILE)
        ]
        top = jnp.concatenate(tops, 1)
        return jnp.concatenate([jnp.exp(part - top).astype(BF16) for part in parts], 1), tops

    def finish(pair, t, probs, tops):
        weights = []
        for j in range(t + 1):
            value = v_ref[j * TILE : (j + 1) * TILE, columns(pair)]
            weights.append(jnp.concatenate([jnp.where(low, value, zero), counters[0]], 1))
            weights.append(jnp.concatenate([jnp.where(low, zero, value), counters[1]], 1))
        both = jnp.dot(probs, jnp.concatenate(weights, 0), preferred_element_type=F32)
        upper, lower = both[:, :PAIR], both[:, PAIR:]
        out_ref[t * TILE : (t + 1) * TILE, columns(pair)] = (upper / lower).astype(BF16)
        if t * TILE % STRIDE == 0:
            a, b = 2 * pair, 2 * pair + 1
            for start, (x, y) in ((0, (upper, upper)), (2, (lower, lower)), (4, tops)):
                row = start + t * TILE // STRIDE
                kept_ref[row : row + 1, columns(pair)] = jnp.where(
                    low, x[a : a + 1], y[b : b + 1]
                )

    ready = [score(0, j) for j in range(TILES)]
    waiting = []
    for pair in range(PAIRS):
        later = []
        for t in range(TILES):
            if pair + 1 < PAIRS:
                later.append(score(pair + 1, t))
            waiting.append((pair, t, *soften(ready, t)))
            if len(waiting) > 1:
                finish(*waiting.pop(0))
        ready = later
    finish(*waiting.pop(0))


def local_level(first, count, arrays, complete):
    spec = pl.BlockSpec((BLOCK, WIDTH), lambda i: (first + i, 0))
    operands = list(arrays)
    in_specs = [spec] * 3
    aliases = {}
    if complete is not None:
        operands.append(complete)
        in_specs.append(pl.BlockSpec(memory_space=pl.ANY))
        aliases = {3: 0}
    return pl.pallas_call(
        local_kernel,
        grid=(count,),
        in_specs=in_specs,
        out_specs=[spec, pl.BlockSpec((8, WIDTH), lambda i: (i, 0))],
        out_shape=[
            jax.ShapeDtypeStruct(arrays[0].shape, BF16),
            jax.ShapeDtypeStruct((8 * count, WIDTH), F32),
        ],
        input_output_aliases=aliases,
        compiler_params=pltpu.CompilerParams(vmem_limit_bytes=LOCAL_VMEM),
        cost_estimate=pl.CostEstimate(
            flops=count * HEADS * 4 * BLOCK * BLOCK * HEAD * 4,
            bytes_accessed=count * 8 * BLOCK * WIDTH,
            transcendentals=count * HEADS * BLOCK * BLOCK,
        ),
        name="local",
    )(*operands)


def merge_kernel(spot_ref, q_ref, own_ref, other_ref, *refs):
    kept_refs, old_ref, out_ref = refs[:-2], refs[-2], refs[-1]
    lanes = HEADS * ROWS
    owned = owner_mask(lanes, ROWS, WIDTH)
    query = q_ref[...] * jnp.asarray(HEAD**-0.5, BF16)
    spread = jnp.where(owned, jnp.concatenate([query] * HEADS, 0), jnp.zeros((), BF16))
    score = jnp.concatenate(
        [
            lax.dot_general(spread, ref[:, :WIDTH], TRANSPOSED, preferred_element_type=F32)
            for ref in (own_ref, other_ref)
        ],
        1,
    )
    keys = score.shape[1]
    device = spot_ref[0]
    column = lax.broadcasted_iota(jnp.int32, (1, keys), 1)
    core, x, z = column // (keys // 2), column // (4 * UNIT) % 4, column // UNIT % 4
    inner = column % UNIT
    quarter = jnp.where(inner < 16, 0, jnp.where(inner < 24, 1, jnp.where(inner < 28, 2, 3)))
    index = jnp.where(
        inner < 16, inner, jnp.where(inner < 24, 2 * (inner - 16), 4 * (inner % 4))
    )
    source = jnp.bitwise_xor(device, quarter * 32 + x * 8 + z * 2 + core)
    key_place = source * ROWS + index
    row = lax.broadcasted_iota(jnp.int32, (lanes, 1), 0) % ROWS
    query_place = device * ROWS + row
    in_one = (quarter == 0).astype(F32)
    in_two = jnp.where((quarter <= 1) & (index % 2 == 0), 1.0, 0.0)
    in_three = jnp.where(index % 4 == 0, 1.0, 0.0)
    has_two = jnp.where(row % 2 == 0, 1.0, 0.0)
    has_three = jnp.where(row % 4 == 0, 1.0, 0.0)
    count = in_one + has_two * in_two + has_three * in_three
    count = jnp.where(key_place <= query_place, count, 0.0)
    score = jnp.where(count > 0.0, score, MASKED)
    top = jnp.max(score, axis=1, keepdims=True)
    probs = jnp.exp(score - top) * count
    total = jnp.sum(probs, axis=1, keepdims=True)
    probs = probs.astype(BF16)
    result = jnp.dot(probs[:, : keys // 2], own_ref[:, WIDTH:], preferred_element_type=F32)
    result = result + jnp.dot(
        probs[:, keys // 2 :], other_ref[:, WIDTH:], preferred_element_type=F32
    )

    def gather_heads(array):
        kept = jnp.where(owned, array, 0.0)
        return jnp.sum(kept.reshape(HEADS, ROWS, WIDTH), axis=0)

    top, total, result = gather_heads(top), gather_heads(total), gather_heads(result)
    blocks = [ref[8 * i : 8 * i + 8] for ref in kept_refs for i in range(ref.shape[0] // 8)]
    result_zero, total_zero, top_zero = (
        jnp.concatenate([block[start : start + 2] for block in blocks], 0) for start in (0, 2, 4)
    )
    best = jnp.maximum(top, top_zero)
    weight, weight_zero = jnp.exp(top - best), jnp.exp(top_zero - best)
    mixed = (weight * result + weight_zero * result_zero) / (
        weight * total + weight_zero * total_zero
    )
    owned = owner_mask(ROWS, 1, WIDTH)
    for i in range(ROWS):
        out_ref[i] = jnp.where(owned, mixed[i : i + 1], old_ref[i].astype(F32)).astype(BF16)


def merge(spot, query, own, other, kept, complete):
    shape = (ROWS, STRIDE, WIDTH)
    corner = pl.BlockSpec((ROWS, ROWS, WIDTH), lambda i: (0, 0, 0))

    def whole(array):
        return pl.BlockSpec(array.shape, lambda i: (0, 0))

    merged = pl.pallas_call(
        merge_kernel,
        grid=(1,),
        in_specs=[pl.BlockSpec(memory_space=pltpu.SMEM)]
        + [whole(array) for array in (query, own, other, *kept)]
        + [corner],
        out_specs=corner,
        out_shape=jax.ShapeDtypeStruct(shape, BF16),
        input_output_aliases={4 + len(kept): 0},
        compiler_params=pltpu.CompilerParams(vmem_limit_bytes=MERGE_VMEM),
        name="merge",
    )(spot, query, own, other, *kept, complete.reshape(shape))
    return merged.reshape(complete.shape)


def local(queries, key_rows, value_rows):
    devices = lax.axis_size("seq")
    arrays = (queries, key_rows, value_rows)

    def exchange(array, distance):
        return lax.ppermute(array, "seq", [(i, i ^ distance) for i in range(devices)])

    query, rows, *sent = pick(*arrays)
    complete, kept, first = None, [], 0
    stages = ((32, 64, 96), (2, 4, 6), (8, 16, 24), (1,))
    for stage, (distances, count) in enumerate(zip(stages, CHUNKS)):
        if stage > 0:
            sent = [rows] * len(distances)
        received = [exchange(part, distance) for part, distance in zip(sent, distances)]
        if count > 0:
            complete, some = local_level(first, count, arrays, complete)
            first += count
            kept.append(some)
            received, rows, complete = lax.optimization_barrier((received, rows, complete))
        if stage == 0:
            rows = jnp.concatenate([rows, received[0], received[1] + received[2]], 0)
        elif stage < 3:
            rows = jnp.concatenate([rows, *received], 0)
        if stage < 3:
            rows, complete, arrays = lax.optimization_barrier((rows, complete, arrays))
    spot = lax.axis_index("seq").astype(jnp.int32).reshape(1)
    return merge(spot, query, rows, received[0], kept, complete)


def solution(mesh):
    in_specs = (P("seq", None), P("seq", None), P("seq", None))
    out_specs = P("seq", None)
    return jax.shard_map(local, mesh=mesh, in_specs=in_specs, out_specs=out_specs, check_vma=False)
```

```python
import jax
import jax.numpy as jnp
from jax import lax
from jax.experimental import pallas as pl
from jax.experimental.pallas import tpu as pltpu
from jax.sharding import PartitionSpec as P

HEADS = 12
HEAD = 64
PAIR = 2 * HEAD
BLOCK = 512
TILE = 128
TILES = BLOCK // TILE
PAIRS = HEADS // 2
WIDTH = HEADS * HEAD
ROWS = 16
STRIDE = 256
UNIT = 2 * ROWS
VMEM = 52 << 20
LOCAL_VMEM = 52 << 20
MERGE_VMEM = 20 << 20

MASKED = -1e30
BF16 = jnp.bfloat16
F32 = jnp.float32
TRANSPOSED = (((1,), (1,)), ((), ()))

CHUNKS = (2, 5, 1)


def owner_mask(rows, row_size, columns):
    row = lax.broadcasted_iota(jnp.int32, (rows, columns), 0) // row_size
    head = lax.broadcasted_iota(jnp.int32, (rows, columns), 1) // HEAD
    return row == head


def pick_kernel(q_ref, k_ref, v_ref, q_out, own_out, second_out, fourth_out):
    owned = owner_mask(ROWS, 1, WIDTH)

    def diagonal(ref):
        return [
            jnp.sum(jnp.where(owned, ref[i].astype(F32), 0.0), axis=0, keepdims=True)
            for i in range(ROWS)
        ]

    def pack(rows):
        return jnp.concatenate(rows, 0).astype(BF16)

    q_out[...] = pack(diagonal(q_ref))
    for ref, columns in ((k_ref, slice(0, WIDTH)), (v_ref, slice(WIDTH, 2 * WIDTH))):
        rows = diagonal(ref)
        none = [jnp.zeros_like(rows[0])] * (ROWS // 4)
        own_out[:, columns] = pack(rows)
        second_out[:, columns] = pack(rows[2::4] + rows[::4])
        fourth_out[:, columns] = pack(rows[::4] + none)


def pick(queries, key_rows, value_rows):
    spec = pl.BlockSpec((ROWS, ROWS, WIDTH), lambda i: (0, 0, 0))
    shape = (ROWS, STRIDE, WIDTH)
    outs = [
        jax.ShapeDtypeStruct(size, BF16)
        for size in ((ROWS, WIDTH), (ROWS, 2 * WIDTH)) + ((ROWS // 2, 2 * WIDTH),) * 2
    ]
    return pl.pallas_call(
        pick_kernel,
        grid=(1,),
        in_specs=[spec] * 3,
        out_specs=[pl.BlockSpec(out.shape, lambda i: (0, 0)) for out in outs],
        out_shape=outs,
        compiler_params=pltpu.CompilerParams(vmem_limit_bytes=VMEM),
        name="pick",
    )(queries.reshape(shape), key_rows.reshape(shape), value_rows.reshape(shape))


def local_kernel(q_ref, k_ref, v_ref, *refs):
    out_ref, kept_ref = refs[-2:]
    low = lax.broadcasted_iota(jnp.int32, (1, PAIR), 1) < HEAD
    keep = lax.broadcasted_iota(
        jnp.int32, (TILE, 2 * TILE), 1
    ) % TILE <= lax.broadcasted_iota(jnp.int32, (TILE, 2 * TILE), 0)
    zero = jnp.zeros((TILE, PAIR), BF16)
    one = jnp.ones((TILE, PAIR), BF16)
    counters = jnp.where(low, one, zero), jnp.where(low, zero, one)

    def columns(pair):
        return slice(pair * PAIR, (pair + 1) * PAIR)

    def score(pair, j):
        query = q_ref[j * TILE :, columns(pair)] * jnp.asarray(HEAD**-0.5, BF16)
        key = k_ref[j * TILE : (j + 1) * TILE, columns(pair)]
        both = jnp.concatenate([jnp.where(low, key, zero), jnp.where(low, zero, key)], 0)
        return lax.dot_general(query, both, TRANSPOSED, preferred_element_type=F32)

    def soften(scores, t):
        parts = [scores[j][(t - j) * TILE : (t - j + 1) * TILE] for j in range(t + 1)]
        parts[t] = jnp.where(keep, parts[t], MASKED)
        most = parts[0]
        for part in parts[1:]:
            most = jnp.maximum(most, part)
        tops = [
            jnp.broadcast_to(
                jnp.max(most[:, start : start + TILE], axis=1, keepdims=True), (TILE, TILE)
            )
            for start in (0, TILE)
        ]
        top = jnp.concatenate(tops, 1)
        return jnp.concatenate([jnp.exp(part - top).astype(BF16) for part in parts], 1), tops

    def finish(pair, t, probs, tops):
        weights = []
        for j in range(t + 1):
            value = v_ref[j * TILE : (j + 1) * TILE, columns(pair)]
            weights.append(jnp.concatenate([jnp.where(low, value, zero), counters[0]], 1))
            weights.append(jnp.concatenate([jnp.where(low, zero, value), counters[1]], 1))
        both = jnp.dot(probs, jnp.concatenate(weights, 0), preferred_element_type=F32)
        upper, lower = both[:, :PAIR], both[:, PAIR:]
        out_ref[t * TILE : (t + 1) * TILE, columns(pair)] = (upper / lower).astype(BF16)
        if t * TILE % STRIDE == 0:
            a, b = 2 * pair, 2 * pair + 1
            for start, (x, y) in ((0, (upper, upper)), (2, (lower, lower)), (4, tops)):
                row = start + t * TILE // STRIDE
                kept_ref[row : row + 1, columns(pair)] = jnp.where(
                    low, x[a : a + 1], y[b : b + 1]
                )

    ready = [score(0, j) for j in range(TILES)]
    waiting = []
    for pair in range(PAIRS):
        later = []
        for t in range(TILES):
            if pair + 1 < PAIRS:
                later.append(score(pair + 1, t))
            waiting.append((pair, t, *soften(ready, t)))
            if len(waiting) > 1:
                finish(*waiting.pop(0))
        ready = later
    finish(*waiting.pop(0))


def local_level(first, count, arrays, complete):
    spec = pl.BlockSpec((BLOCK, WIDTH), lambda i: (first + i, 0))
    operands = list(arrays)
    in_specs = [spec] * 3
    aliases = {}
    if complete is not None:
        operands.append(complete)
        in_specs.append(pl.BlockSpec(memory_space=pl.ANY))
        aliases = {3: 0}
    return pl.pallas_call(
        local_kernel,
        grid=(count,),
        in_specs=in_specs,
        out_specs=[spec, pl.BlockSpec((8, WIDTH), lambda i: (i, 0))],
        out_shape=[
            jax.ShapeDtypeStruct(arrays[0].shape, BF16),
            jax.ShapeDtypeStruct((8 * count, WIDTH), F32),
        ],
        input_output_aliases=aliases,
        compiler_params=pltpu.CompilerParams(vmem_limit_bytes=LOCAL_VMEM),
        cost_estimate=pl.CostEstimate(
            flops=count * HEADS * 4 * BLOCK * BLOCK * HEAD * 4,
            bytes_accessed=count * 8 * BLOCK * WIDTH,
            transcendentals=count * HEADS * BLOCK * BLOCK,
        ),
        name="local",
    )(*operands)


def merge_kernel(spot_ref, q_ref, own_ref, other_ref, *refs):
    kept_refs, old_ref, out_ref, corner, sems = refs[:-5], refs[-5], refs[-4], refs[-3], refs[-2:]
    old = pltpu.make_async_copy(old_ref.at[:, pl.ds(0, ROWS), :], corner, sems[0])
    old.start()
    lanes = HEADS * ROWS
    owned = owner_mask(lanes, ROWS, WIDTH)
    query = q_ref[...] * jnp.asarray(HEAD**-0.5, BF16)
    spread = jnp.where(owned, jnp.concatenate([query] * HEADS, 0), jnp.zeros((), BF16))
    score = jnp.concatenate(
        [
            lax.dot_general(spread, ref[:, :WIDTH], TRANSPOSED, preferred_element_type=F32)
            for ref in (own_ref, other_ref)
        ],
        1,
    )
    keys = score.shape[1]
    device = spot_ref[0]
    column = lax.broadcasted_iota(jnp.int32, (1, keys), 1)
    core, x, z = column // (keys // 2), column // (4 * UNIT) % 4, column // UNIT % 4
    inner = column % UNIT
    quarter = jnp.where(inner < 16, 0, jnp.where(inner < 24, 1, jnp.where(inner < 28, 3, 2)))
    index = jnp.where(
        inner < 16, inner, 4 * (inner % 4) + jnp.where((inner >= 16) & (inner < 20), 2, 0)
    )
    source = jnp.bitwise_xor(device, quarter * 32 + x * 8 + z * 2 + core)
    key_place = source * ROWS + index
    row = lax.broadcasted_iota(jnp.int32, (lanes, 1), 0) % ROWS
    query_place = device * ROWS + row
    in_one = (quarter == 0).astype(F32)
    in_two = jnp.where((quarter <= 1) & (index % 2 == 0), 1.0, 0.0)
    in_three = jnp.where(index % 4 == 0, 1.0, 0.0)
    has_two = jnp.where(row % 2 == 0, 1.0, 0.0)
    has_three = jnp.where(row % 4 == 0, 1.0, 0.0)
    count = in_one + has_two * in_two + has_three * in_three
    count = jnp.where(key_place <= query_place, count, 0.0)
    score = jnp.where(count > 0.0, score, MASKED)
    top = jnp.max(score, axis=1, keepdims=True)
    probs = jnp.exp(score - top) * count
    total = jnp.sum(probs, axis=1, keepdims=True)
    probs = probs.astype(BF16)
    result = jnp.dot(probs[:, : keys // 2], own_ref[:, WIDTH:], preferred_element_type=F32)
    result = result + jnp.dot(
        probs[:, keys // 2 :], other_ref[:, WIDTH:], preferred_element_type=F32
    )

    def gather_heads(array):
        kept = jnp.where(owned, array, 0.0)
        return jnp.sum(kept.reshape(HEADS, ROWS, WIDTH), axis=0)

    top, total, result = gather_heads(top), gather_heads(total), gather_heads(result)
    blocks = [ref[8 * i : 8 * i + 8] for ref in kept_refs for i in range(ref.shape[0] // 8)]
    result_zero, total_zero, top_zero = (
        jnp.concatenate([block[start : start + 2] for block in blocks], 0) for start in (0, 2, 4)
    )
    best = jnp.maximum(top, top_zero)
    weight, weight_zero = jnp.exp(top - best), jnp.exp(top_zero - best)
    mixed = (weight * result + weight_zero * result_zero) / (
        weight * total + weight_zero * total_zero
    )
    owned = owner_mask(ROWS, 1, WIDTH)
    old.wait()
    for i in range(ROWS):
        corner[i] = jnp.where(owned, mixed[i : i + 1], corner[i].astype(F32)).astype(BF16)
    new = pltpu.make_async_copy(corner, out_ref.at[:, pl.ds(0, ROWS), :], sems[1])
    new.start()
    new.wait()


def merge(spot, query, own, other, kept, complete):
    shape = (ROWS, STRIDE, WIDTH)
    held = pl.BlockSpec(memory_space=pltpu.VMEM)
    anywhere = pl.BlockSpec(memory_space=pl.ANY)
    merged = pl.pallas_call(
        merge_kernel,
        in_specs=[pl.BlockSpec(memory_space=pltpu.SMEM)] + [held] * (3 + len(kept)) + [anywhere],
        out_specs=anywhere,
        out_shape=jax.ShapeDtypeStruct(shape, BF16),
        input_output_aliases={4 + len(kept): 0},
        scratch_shapes=[
            pltpu.VMEM((ROWS, ROWS, WIDTH), BF16),
            pltpu.SemaphoreType.DMA,
            pltpu.SemaphoreType.DMA,
        ],
        compiler_params=pltpu.CompilerParams(vmem_limit_bytes=MERGE_VMEM),
        name="merge",
    )(spot, query, own, other, *kept, complete.reshape(shape))
    return merged.reshape(complete.shape)


def local(queries, key_rows, value_rows):
    devices = lax.axis_size("seq")
    arrays = (queries, key_rows, value_rows)

    def exchange(array, distance):
        return lax.ppermute(array, "seq", [(i, i ^ distance) for i in range(devices)])

    query, rows, second, fourth = pick(*arrays)
    near = exchange(second, 32)
    own = lax.broadcasted_iota(jnp.int32, second.shape, 0) < ROWS // 4
    far = exchange(jnp.where(own, fourth, near), 96)
    rows = jnp.concatenate([rows, near, far], 0)
    complete, kept, first = None, [], 0
    for stage, (distances, count) in enumerate(zip(((2, 4, 6), (8, 16, 24), (1,)), CHUNKS)):
        rows, complete, arrays = lax.optimization_barrier((rows, complete, arrays))
        received = [exchange(rows, distance) for distance in distances]
        complete, some = local_level(first, count, arrays, complete)
        first += count
        kept.append(some)
        received, rows, complete = lax.optimization_barrier((received, rows, complete))
        if stage < 2:
            rows = jnp.concatenate([rows, *received], 0)
    spot = lax.axis_index("seq").astype(jnp.int32).reshape(1)
    return merge(spot, query, rows, received[0], kept, complete)


def solution(mesh):
    in_specs = (P("seq", None), P("seq", None), P("seq", None))
    out_specs = P("seq", None)
    return jax.shard_map(local, mesh=mesh, in_specs=in_specs, out_specs=out_specs, check_vma=False)
```

```python
import jax
import jax.numpy as jnp
from jax import lax
from jax.experimental import pallas as pl
from jax.experimental.pallas import tpu as pltpu
from jax.sharding import PartitionSpec as P

HEADS = 12
HEAD = 64
PAIR = 2 * HEAD
BLOCK = 512
TILE = 128
TILES = BLOCK // TILE
PAIRS = HEADS // 2
WIDTH = HEADS * HEAD
ROWS = 16
STRIDE = 256
UNIT = 2 * ROWS
VMEM = 52 << 20
LOCAL_VMEM = 52 << 20
MERGE_VMEM = 20 << 20

MASKED = -1e30
BF16 = jnp.bfloat16
F32 = jnp.float32
TRANSPOSED = (((1,), (1,)), ((), ()))

CHUNKS = (1, 1, 5, 1)


def owner_mask(rows, row_size, columns):
    row = lax.broadcasted_iota(jnp.int32, (rows, columns), 0) // row_size
    head = lax.broadcasted_iota(jnp.int32, (rows, columns), 1) // HEAD
    return row == head


def pick_kernel(q_ref, k_ref, v_ref, q_out, own_out, second_out, low_out, high_out):
    owned = owner_mask(ROWS, 1, WIDTH)

    def diagonal(ref):
        return [
            jnp.sum(jnp.where(owned, ref[i].astype(F32), 0.0), axis=0, keepdims=True)
            for i in range(ROWS)
        ]

    def pack(rows):
        return jnp.concatenate(rows, 0).astype(BF16)

    q_out[...] = pack(diagonal(q_ref))
    for ref, columns in ((k_ref, slice(0, WIDTH)), (v_ref, slice(WIDTH, 2 * WIDTH))):
        rows = diagonal(ref)
        none = [jnp.zeros_like(rows[0])] * (ROWS // 4)
        own_out[:, columns] = pack(rows)
        second_out[:, columns] = pack(rows[::2])
        low_out[:, columns] = pack(rows[::4] + none)
        high_out[:, columns] = pack(none + rows[::4])


def pick(queries, key_rows, value_rows):
    spec = pl.BlockSpec((ROWS, ROWS, WIDTH), lambda i: (0, 0, 0))
    shape = (ROWS, STRIDE, WIDTH)
    outs = [
        jax.ShapeDtypeStruct(size, BF16)
        for size in ((ROWS, WIDTH), (ROWS, 2 * WIDTH)) + ((ROWS // 2, 2 * WIDTH),) * 3
    ]
    return pl.pallas_call(
        pick_kernel,
        grid=(1,),
        in_specs=[spec] * 3,
        out_specs=[pl.BlockSpec(out.shape, lambda i: (0, 0)) for out in outs],
        out_shape=outs,
        compiler_params=pltpu.CompilerParams(vmem_limit_bytes=VMEM),
        name="pick",
    )(queries.reshape(shape), key_rows.reshape(shape), value_rows.reshape(shape))


def local_kernel(q_ref, k_ref, v_ref, *refs):
    out_ref, kept_ref = refs[-2:]
    low = lax.broadcasted_iota(jnp.int32, (1, PAIR), 1) < HEAD
    keep = lax.broadcasted_iota(
        jnp.int32, (TILE, 2 * TILE), 1
    ) % TILE <= lax.broadcasted_iota(jnp.int32, (TILE, 2 * TILE), 0)
    zero = jnp.zeros((TILE, PAIR), BF16)
    one = jnp.ones((TILE, PAIR), BF16)
    counters = jnp.where(low, one, zero), jnp.where(low, zero, one)

    def columns(pair):
        return slice(pair * PAIR, (pair + 1) * PAIR)

    def score(pair, j):
        query = q_ref[j * TILE :, columns(pair)] * jnp.asarray(HEAD**-0.5, BF16)
        key = k_ref[j * TILE : (j + 1) * TILE, columns(pair)]
        both = jnp.concatenate([jnp.where(low, key, zero), jnp.where(low, zero, key)], 0)
        return lax.dot_general(query, both, TRANSPOSED, preferred_element_type=F32)

    def soften(scores, t):
        parts = [scores[j][(t - j) * TILE : (t - j + 1) * TILE] for j in range(t + 1)]
        parts[t] = jnp.where(keep, parts[t], MASKED)
        most = parts[0]
        for part in parts[1:]:
            most = jnp.maximum(most, part)
        tops = [
            jnp.broadcast_to(
                jnp.max(most[:, start : start + TILE], axis=1, keepdims=True), (TILE, TILE)
            )
            for start in (0, TILE)
        ]
        top = jnp.concatenate(tops, 1)
        return jnp.concatenate([jnp.exp(part - top).astype(BF16) for part in parts], 1), tops

    def finish(pair, t, probs, tops):
        weights = []
        for j in range(t + 1):
            value = v_ref[j * TILE : (j + 1) * TILE, columns(pair)]
            weights.append(jnp.concatenate([jnp.where(low, value, zero), counters[0]], 1))
            weights.append(jnp.concatenate([jnp.where(low, zero, value), counters[1]], 1))
        both = jnp.dot(probs, jnp.concatenate(weights, 0), preferred_element_type=F32)
        upper, lower = both[:, :PAIR], both[:, PAIR:]
        out_ref[t * TILE : (t + 1) * TILE, columns(pair)] = (upper / lower).astype(BF16)
        if t * TILE % STRIDE == 0:
            a, b = 2 * pair, 2 * pair + 1
            for start, (x, y) in ((0, (upper, upper)), (2, (lower, lower)), (4, tops)):
                row = start + t * TILE // STRIDE
                kept_ref[row : row + 1, columns(pair)] = jnp.where(
                    low, x[a : a + 1], y[b : b + 1]
                )

    ready = [score(0, j) for j in range(TILES)]
    waiting = []
    for pair in range(PAIRS):
        later = []
        for t in range(TILES):
            if pair + 1 < PAIRS:
                later.append(score(pair + 1, t))
            waiting.append((pair, t, *soften(ready, t)))
            if len(waiting) > 1:
                finish(*waiting.pop(0))
        ready = later
    finish(*waiting.pop(0))


def local_level(first, count, arrays, complete):
    spec = pl.BlockSpec((BLOCK, WIDTH), lambda i: (first + i, 0))
    operands = list(arrays)
    in_specs = [spec] * 3
    aliases = {}
    if complete is not None:
        operands.append(complete)
        in_specs.append(pl.BlockSpec(memory_space=pl.ANY))
        aliases = {3: 0}
    return pl.pallas_call(
        local_kernel,
        grid=(count,),
        in_specs=in_specs,
        out_specs=[spec, pl.BlockSpec((8, WIDTH), lambda i: (i, 0))],
        out_shape=[
            jax.ShapeDtypeStruct(arrays[0].shape, BF16),
            jax.ShapeDtypeStruct((8 * count, WIDTH), F32),
        ],
        input_output_aliases=aliases,
        compiler_params=pltpu.CompilerParams(vmem_limit_bytes=LOCAL_VMEM),
        cost_estimate=pl.CostEstimate(
            flops=count * HEADS * 4 * BLOCK * BLOCK * HEAD * 4,
            bytes_accessed=count * 8 * BLOCK * WIDTH,
            transcendentals=count * HEADS * BLOCK * BLOCK,
        ),
        name="local",
    )(*operands)


def merge_kernel(spot_ref, q_ref, own_ref, other_ref, *refs):
    kept_refs, old_ref, out_ref, corner, sems = refs[:-5], refs[-5], refs[-4], refs[-3], refs[-2:]
    old = pltpu.make_async_copy(old_ref.at[:, pl.ds(0, ROWS), :], corner, sems[0])
    old.start()
    lanes = HEADS * ROWS
    owned = owner_mask(lanes, ROWS, WIDTH)
    query = q_ref[...] * jnp.asarray(HEAD**-0.5, BF16)
    spread = jnp.where(owned, jnp.concatenate([query] * HEADS, 0), jnp.zeros((), BF16))
    score = jnp.concatenate(
        [
            lax.dot_general(spread, ref[:, :WIDTH], TRANSPOSED, preferred_element_type=F32)
            for ref in (own_ref, other_ref)
        ],
        1,
    )
    keys = score.shape[1]
    device = spot_ref[0]
    column = lax.broadcasted_iota(jnp.int32, (1, keys), 1)
    core, x, z = column // (keys // 2), column // (4 * UNIT) % 4, column // UNIT % 4
    inner = column % UNIT
    quarter = jnp.where(inner < 16, 0, jnp.where(inner < 24, 1, jnp.where(inner < 28, 2, 3)))
    index = jnp.where(
        inner < 16, inner, jnp.where(inner < 24, 2 * (inner - 16), 4 * (inner % 4))
    )
    source = jnp.bitwise_xor(device, quarter * 32 + x * 8 + z * 2 + core)
    key_place = source * ROWS + index
    row = lax.broadcasted_iota(jnp.int32, (lanes, 1), 0) % ROWS
    query_place = device * ROWS + row
    in_one = (quarter == 0).astype(F32)
    in_two = jnp.where((quarter <= 1) & (index % 2 == 0), 1.0, 0.0)
    in_three = jnp.where(index % 4 == 0, 1.0, 0.0)
    has_two = jnp.where(row % 2 == 0, 1.0, 0.0)
    has_three = jnp.where(row % 4 == 0, 1.0, 0.0)
    count = in_one + has_two * in_two + has_three * in_three
    count = jnp.where(key_place <= query_place, count, 0.0)
    score = jnp.where(count > 0.0, score, MASKED)
    top = jnp.max(score, axis=1, keepdims=True)
    probs = jnp.exp(score - top) * count
    total = jnp.sum(probs, axis=1, keepdims=True)
    probs = probs.astype(BF16)
    result = jnp.dot(probs[:, : keys // 2], own_ref[:, WIDTH:], preferred_element_type=F32)
    result = result + jnp.dot(
        probs[:, keys // 2 :], other_ref[:, WIDTH:], preferred_element_type=F32
    )

    def gather_heads(array):
        kept = jnp.where(owned, array, 0.0)
        return jnp.sum(kept.reshape(HEADS, ROWS, WIDTH), axis=0)

    top, total, result = gather_heads(top), gather_heads(total), gather_heads(result)
    blocks = [ref[8 * i : 8 * i + 8] for ref in kept_refs for i in range(ref.shape[0] // 8)]
    result_zero, total_zero, top_zero = (
        jnp.concatenate([block[start : start + 2] for block in blocks], 0) for start in (0, 2, 4)
    )
    best = jnp.maximum(top, top_zero)
    weight, weight_zero = jnp.exp(top - best), jnp.exp(top_zero - best)
    mixed = (weight * result + weight_zero * result_zero) / (
        weight * total + weight_zero * total_zero
    )
    owned = owner_mask(ROWS, 1, WIDTH)
    old.wait()
    for i in range(ROWS):
        corner[i] = jnp.where(owned, mixed[i : i + 1], corner[i].astype(F32)).astype(BF16)
    new = pltpu.make_async_copy(corner, out_ref.at[:, pl.ds(0, ROWS), :], sems[1])
    new.start()
    new.wait()


def merge(spot, query, own, other, kept, complete):
    shape = (ROWS, STRIDE, WIDTH)
    held = pl.BlockSpec(memory_space=pltpu.VMEM)
    anywhere = pl.BlockSpec(memory_space=pl.ANY)
    merged = pl.pallas_call(
        merge_kernel,
        in_specs=[pl.BlockSpec(memory_space=pltpu.SMEM)] + [held] * (3 + len(kept)) + [anywhere],
        out_specs=anywhere,
        out_shape=jax.ShapeDtypeStruct(shape, BF16),
        input_output_aliases={4 + len(kept): 0},
        scratch_shapes=[
            pltpu.VMEM((ROWS, ROWS, WIDTH), BF16),
            pltpu.SemaphoreType.DMA,
            pltpu.SemaphoreType.DMA,
        ],
        compiler_params=pltpu.CompilerParams(vmem_limit_bytes=MERGE_VMEM),
        name="merge",
    )(spot, query, own, other, *kept, complete.reshape(shape))
    return merged.reshape(complete.shape)


def local(queries, key_rows, value_rows):
    devices = lax.axis_size("seq")
    arrays = (queries, key_rows, value_rows)

    def exchange(array, distance):
        return lax.ppermute(array, "seq", [(i, i ^ distance) for i in range(devices)])

    query, rows, *sent = pick(*arrays)
    complete, kept, first = None, [], 0
    stages = ((32, 64, 96), (2, 4, 6), (8, 16, 24), (1,))
    for stage, (distances, count) in enumerate(zip(stages, CHUNKS)):
        if stage > 0:
            sent = [rows] * len(distances)
        received = [exchange(part, distance) for part, distance in zip(sent, distances)]
        complete, some = local_level(first, count, arrays, complete)
        first += count
        kept.append(some)
        received, rows, complete = lax.optimization_barrier((received, rows, complete))
        if stage == 0:
            rows = jnp.concatenate([rows, received[0], received[1] + received[2]], 0)
        elif stage < 3:
            rows = jnp.concatenate([rows, *received], 0)
        if stage < 3:
            rows, complete, arrays = lax.optimization_barrier((rows, complete, arrays))
    spot = lax.axis_index("seq").astype(jnp.int32).reshape(1)
    return merge(spot, query, rows, received[0], kept, complete)


def solution(mesh):
    in_specs = (P("seq", None), P("seq", None), P("seq", None))
    out_specs = P("seq", None)
    return jax.shard_map(local, mesh=mesh, in_specs=in_specs, out_specs=out_specs, check_vma=False)
```

```python
import functools

import jax
import jax.numpy as jnp
from jax import lax
from jax.experimental import pallas as pl
from jax.experimental.pallas import tpu as pltpu
from jax.sharding import PartitionSpec as P

HEADS = 12
HEAD = 64
PAIR = 2 * HEAD
BLOCK = 512
TILE = 128
TILES = BLOCK // TILE
PAIRS = HEADS // 2
WIDTH = HEADS * HEAD
ROWS = 16
STRIDE = 256
UNIT = 2 * ROWS
PICK_VMEM = 50 << 20
LOCAL_VMEM = 52 << 20
MERGE_VMEM = 20 << 20
SINGLE_VMEM = 48 << 20

MASKED = -1e30
BF16 = jnp.bfloat16
F32 = jnp.float32
TRANSPOSED = (((1,), (1,)), ((), ()))

CHUNKS = (1, 1, 5, 1)
GROUPS = ((0, 3), (3, 5), (5, 6))


def owner_mask(rows, row_size, columns):
    row = lax.broadcasted_iota(jnp.int32, (rows, columns), 0) // row_size
    head = lax.broadcasted_iota(jnp.int32, (rows, columns), 1) // HEAD
    return row == head


def fetch_block(block, sources, targets, sems):
    rows = pl.ds(block * BLOCK, BLOCK)
    return [
        pltpu.make_async_copy(source.at[rows, :], target, sems.at[i])
        for i, (source, target) in enumerate(zip(sources, targets))
    ]


def pick_kernel(
    q_all, k_all, v_all, q_hbm, k_hbm, v_hbm, q_out, own_out, second_out, low_out, high_out, *refs
):
    targets, (q_ref, k_ref, v_ref), (corner_sems, block_sems) = refs[:3], refs[3:6], refs[6:]
    corners = [
        pltpu.make_async_copy(source.at[:, pl.ds(0, ROWS), :], target, corner_sems.at[i])
        for i, (source, target) in enumerate(
            ((q_all, q_ref), (k_all, k_ref), (v_all, v_ref))
        )
    ]
    blocks = fetch_block(0, (q_hbm, k_hbm, v_hbm), targets, block_sems)
    for copy in corners + blocks:
        copy.start()
    for copy in corners:
        copy.wait()
    owned = owner_mask(ROWS, 1, WIDTH)

    def diagonal(ref):
        return [
            jnp.sum(jnp.where(owned, ref[i].astype(F32), 0.0), axis=0, keepdims=True)
            for i in range(ROWS)
        ]

    def pack(rows):
        return jnp.concatenate(rows, 0).astype(BF16)

    q_out[...] = pack(diagonal(q_ref))
    for ref, columns in ((k_ref, slice(0, WIDTH)), (v_ref, slice(WIDTH, 2 * WIDTH))):
        rows = diagonal(ref)
        none = [jnp.zeros_like(rows[0])] * (ROWS // 4)
        own_out[:, columns] = pack(rows)
        second_out[:, columns] = pack(rows[::2])
        low_out[:, columns] = pack(rows[::4] + none)
        high_out[:, columns] = pack(none + rows[::4])
    for copy in blocks:
        copy.wait()


def pick(queries, key_rows, value_rows):
    arrays = (queries, key_rows, value_rows)
    shape = (ROWS, STRIDE, WIDTH)
    sizes = ((ROWS, WIDTH), (ROWS, 2 * WIDTH)) + ((ROWS // 2, 2 * WIDTH),) * 3
    sizes = sizes + ((BLOCK, WIDTH),) * 3
    return pl.pallas_call(
        pick_kernel,
        in_specs=[pl.BlockSpec(memory_space=pl.ANY)] * 6,
        out_specs=[pl.BlockSpec(memory_space=pltpu.VMEM)] * len(sizes),
        out_shape=[jax.ShapeDtypeStruct(size, BF16) for size in sizes],
        scratch_shapes=[pltpu.VMEM((ROWS, ROWS, WIDTH), BF16)] * 3
        + [pltpu.SemaphoreType.DMA((3,))] * 2,
        compiler_params=pltpu.CompilerParams(vmem_limit_bytes=PICK_VMEM),
        name="pick",
    )(*(array.reshape(shape) for array in arrays), *arrays)


def attend_block(q_ref, k_ref, v_ref, out_ref, kept_ref, after=lambda pair: None):
    low = lax.broadcasted_iota(jnp.int32, (1, PAIR), 1) < HEAD
    keep = lax.broadcasted_iota(
        jnp.int32, (TILE, 2 * TILE), 1
    ) % TILE <= lax.broadcasted_iota(jnp.int32, (TILE, 2 * TILE), 0)
    zero = jnp.zeros((TILE, PAIR), BF16)
    one = jnp.ones((TILE, PAIR), BF16)
    counters = jnp.where(low, one, zero), jnp.where(low, zero, one)

    def columns(pair):
        return slice(pair * PAIR, (pair + 1) * PAIR)

    def score(pair, j):
        query = q_ref[j * TILE :, columns(pair)] * jnp.asarray(HEAD**-0.5, BF16)
        key = k_ref[j * TILE : (j + 1) * TILE, columns(pair)]
        both = jnp.concatenate([jnp.where(low, key, zero), jnp.where(low, zero, key)], 0)
        return lax.dot_general(query, both, TRANSPOSED, preferred_element_type=F32)

    def soften(scores, t):
        parts = [scores[j][(t - j) * TILE : (t - j + 1) * TILE] for j in range(t + 1)]
        parts[t] = jnp.where(keep, parts[t], MASKED)
        most = parts[0]
        for part in parts[1:]:
            most = jnp.maximum(most, part)
        tops = [
            jnp.broadcast_to(
                jnp.max(most[:, start : start + TILE], axis=1, keepdims=True), (TILE, TILE)
            )
            for start in (0, TILE)
        ]
        top = jnp.concatenate(tops, 1)
        return jnp.concatenate([jnp.exp(part - top).astype(BF16) for part in parts], 1), tops

    def finish(pair, t, probs, tops):
        weights = []
        for j in range(t + 1):
            value = v_ref[j * TILE : (j + 1) * TILE, columns(pair)]
            weights.append(jnp.concatenate([jnp.where(low, value, zero), counters[0]], 1))
            weights.append(jnp.concatenate([jnp.where(low, zero, value), counters[1]], 1))
        both = jnp.dot(probs, jnp.concatenate(weights, 0), preferred_element_type=F32)
        upper, lower = both[:, :PAIR], both[:, PAIR:]
        out_ref[t * TILE : (t + 1) * TILE, columns(pair)] = (upper / lower).astype(BF16)
        if t * TILE % STRIDE == 0:
            a, b = 2 * pair, 2 * pair + 1
            for start, (x, y) in ((0, (upper, upper)), (2, (lower, lower)), (4, tops)):
                row = start + t * TILE // STRIDE
                kept_ref[row : row + 1, columns(pair)] = jnp.where(
                    low, x[a : a + 1], y[b : b + 1]
                )
        if t == TILES - 1:
            after(pair)

    ready = [score(0, j) for j in range(TILES)]
    waiting = []
    for pair in range(PAIRS):
        later = []
        for t in range(TILES):
            if pair + 1 < PAIRS:
                later.append(score(pair + 1, t))
            waiting.append((pair, t, *soften(ready, t)))
            if len(waiting) > 1:
                finish(*waiting.pop(0))
        ready = later
    finish(*waiting.pop(0))


def local_kernel(q_ref, k_ref, v_ref, *refs):
    attend_block(q_ref, k_ref, v_ref, *refs[-2:])


def single_kernel(first, following, q_ref, k_ref, v_ref, *refs):
    fetched = 0 if following is None else 3
    sources, refs = refs[:fetched], refs[-(5 + fetched) :]
    out_hbm, kept_ref, targets = refs[0], refs[1], refs[2 : 2 + fetched]
    out_ref, out_sems, block_sems = refs[2 + fetched :]
    blocks = fetch_block(following, sources, targets, block_sems) if fetched else []
    for copy in blocks:
        copy.start()

    def write(group):
        columns = pl.ds(group[0] * PAIR, (group[1] - group[0]) * PAIR)
        return pltpu.make_async_copy(
            out_ref.at[:, columns],
            out_hbm.at[pl.ds(first * BLOCK, BLOCK), columns],
            out_sems.at[GROUPS.index(group)],
        )

    def after(pair):
        for group in GROUPS:
            if group[1] == pair + 1:
                write(group).start()

    attend_block(q_ref, k_ref, v_ref, out_ref, kept_ref, after)
    for copy in [write(group) for group in GROUPS] + blocks:
        copy.wait()


def costs(count):
    return pl.CostEstimate(
        flops=count * HEADS * 4 * BLOCK * BLOCK * HEAD * 4,
        bytes_accessed=count * 8 * BLOCK * WIDTH,
        transcendentals=count * HEADS * BLOCK * BLOCK,
    )


def single_level(first, following, held, arrays, complete):
    anywhere = pl.BlockSpec(memory_space=pl.ANY)
    vmem = pl.BlockSpec(memory_space=pltpu.VMEM)
    operands = list(held)
    fetched = 0
    if following is not None:
        operands.extend(arrays)
        fetched = 3
    aliases = {}
    if complete is not None:
        aliases = {len(operands): 0}
        operands.append(complete)
    complete, kept, *held = pl.pallas_call(
        functools.partial(single_kernel, first, following),
        in_specs=[vmem] * 3 + [anywhere] * (len(operands) - 3),
        out_specs=[anywhere, vmem] + [vmem] * fetched,
        out_shape=[
            jax.ShapeDtypeStruct(arrays[0].shape, BF16),
            jax.ShapeDtypeStruct((8, WIDTH), F32),
        ]
        + [jax.ShapeDtypeStruct((BLOCK, WIDTH), BF16)] * fetched,
        input_output_aliases=aliases,
        scratch_shapes=[
            pltpu.VMEM((BLOCK, WIDTH), BF16),
            pltpu.SemaphoreType.DMA((len(GROUPS),)),
            pltpu.SemaphoreType.DMA((3,)),
        ],
        compiler_params=pltpu.CompilerParams(vmem_limit_bytes=SINGLE_VMEM),
        cost_estimate=costs(1),
        name="single",
    )(*operands)
    return complete, kept, held


def local_level(first, count, arrays, complete):
    spec = pl.BlockSpec((BLOCK, WIDTH), lambda i: (first + i, 0))
    operands = list(arrays)
    in_specs = [spec] * 3
    aliases = {}
    if complete is not None:
        operands.append(complete)
        in_specs.append(pl.BlockSpec(memory_space=pl.ANY))
        aliases = {3: 0}
    return pl.pallas_call(
        local_kernel,
        grid=(count,),
        in_specs=in_specs,
        out_specs=[spec, pl.BlockSpec((8, WIDTH), lambda i: (i, 0))],
        out_shape=[
            jax.ShapeDtypeStruct(arrays[0].shape, BF16),
            jax.ShapeDtypeStruct((8 * count, WIDTH), F32),
        ],
        input_output_aliases=aliases,
        compiler_params=pltpu.CompilerParams(vmem_limit_bytes=LOCAL_VMEM),
        cost_estimate=costs(count),
        name="local",
    )(*operands)


def merge_kernel(spot_ref, q_ref, own_ref, other_ref, *refs):
    kept_refs, old_ref, out_ref, corner, sems = refs[:-5], refs[-5], refs[-4], refs[-3], refs[-2:]
    old = pltpu.make_async_copy(old_ref.at[:, pl.ds(0, ROWS), :], corner, sems[0])
    old.start()
    lanes = HEADS * ROWS
    owned = owner_mask(lanes, ROWS, WIDTH)
    query = q_ref[...] * jnp.asarray(HEAD**-0.5, BF16)
    spread = jnp.where(owned, jnp.concatenate([query] * HEADS, 0), jnp.zeros((), BF16))
    score = jnp.concatenate(
        [
            lax.dot_general(spread, ref[:, :WIDTH], TRANSPOSED, preferred_element_type=F32)
            for ref in (own_ref, other_ref)
        ],
        1,
    )
    keys = score.shape[1]
    device = spot_ref[0]
    column = lax.broadcasted_iota(jnp.int32, (1, keys), 1)
    core, x, z = column // (keys // 2), column // (4 * UNIT) % 4, column // UNIT % 4
    inner = column % UNIT
    quarter = jnp.where(inner < 16, 0, jnp.where(inner < 24, 1, jnp.where(inner < 28, 2, 3)))
    index = jnp.where(
        inner < 16, inner, jnp.where(inner < 24, 2 * (inner - 16), 4 * (inner % 4))
    )
    source = jnp.bitwise_xor(device, quarter * 32 + x * 8 + z * 2 + core)
    key_place = source * ROWS + index
    row = lax.broadcasted_iota(jnp.int32, (lanes, 1), 0) % ROWS
    query_place = device * ROWS + row
    in_one = (quarter == 0).astype(F32)
    in_two = jnp.where((quarter <= 1) & (index % 2 == 0), 1.0, 0.0)
    in_three = jnp.where(index % 4 == 0, 1.0, 0.0)
    has_two = jnp.where(row % 2 == 0, 1.0, 0.0)
    has_three = jnp.where(row % 4 == 0, 1.0, 0.0)
    count = in_one + has_two * in_two + has_three * in_three
    count = jnp.where(key_place <= query_place, count, 0.0)
    score = jnp.where(count > 0.0, score, MASKED)
    top = jnp.max(score, axis=1, keepdims=True)
    probs = jnp.exp(score - top) * count
    total = jnp.sum(probs, axis=1, keepdims=True)
    probs = probs.astype(BF16)
    result = jnp.dot(probs[:, : keys // 2], own_ref[:, WIDTH:], preferred_element_type=F32)
    result = result + jnp.dot(
        probs[:, keys // 2 :], other_ref[:, WIDTH:], preferred_element_type=F32
    )

    def gather_heads(array):
        kept = jnp.where(owned, array, 0.0)
        return jnp.sum(kept.reshape(HEADS, ROWS, WIDTH), axis=0)

    top, total, result = gather_heads(top), gather_heads(total), gather_heads(result)
    blocks = [ref[8 * i : 8 * i + 8] for ref in kept_refs for i in range(ref.shape[0] // 8)]
    result_zero, total_zero, top_zero = (
        jnp.concatenate([block[start : start + 2] for block in blocks], 0) for start in (0, 2, 4)
    )
    best = jnp.maximum(top, top_zero)
    weight, weight_zero = jnp.exp(top - best), jnp.exp(top_zero - best)
    mixed = (weight * result + weight_zero * result_zero) / (
        weight * total + weight_zero * total_zero
    )
    owned = owner_mask(ROWS, 1, WIDTH)
    old.wait()
    for i in range(ROWS):
        corner[i] = jnp.where(owned, mixed[i : i + 1], corner[i].astype(F32)).astype(BF16)
    new = pltpu.make_async_copy(corner, out_ref.at[:, pl.ds(0, ROWS), :], sems[1])
    new.start()
    new.wait()


def merge(spot, query, own, other, kept, complete):
    shape = (ROWS, STRIDE, WIDTH)
    held = pl.BlockSpec(memory_space=pltpu.VMEM)
    anywhere = pl.BlockSpec(memory_space=pl.ANY)
    merged = pl.pallas_call(
        merge_kernel,
        in_specs=[pl.BlockSpec(memory_space=pltpu.SMEM)] + [held] * (3 + len(kept)) + [anywhere],
        out_specs=anywhere,
        out_shape=jax.ShapeDtypeStruct(shape, BF16),
        input_output_aliases={4 + len(kept): 0},
        scratch_shapes=[
            pltpu.VMEM((ROWS, ROWS, WIDTH), BF16),
            pltpu.SemaphoreType.DMA,
            pltpu.SemaphoreType.DMA,
        ],
        compiler_params=pltpu.CompilerParams(vmem_limit_bytes=MERGE_VMEM),
        name="merge",
    )(spot, query, own, other, *kept, complete.reshape(shape))
    return merged.reshape(complete.shape)


def local(queries, key_rows, value_rows):
    devices = lax.axis_size("seq")
    arrays = (queries, key_rows, value_rows)

    def exchange(array, distance):
        return lax.ppermute(array, "seq", [(i, i ^ distance) for i in range(devices)])

    query, rows, near, low, high, *held = pick(*arrays)
    sent = [near, low, high]
    last = sum(CHUNKS) - 1
    complete, kept, first = None, [], 0
    stages = ((32, 64, 96), (2, 4, 6), (8, 16, 24), (1,))
    for stage, (distances, count) in enumerate(zip(stages, CHUNKS)):
        if stage > 0:
            sent = [rows] * len(distances)
        received = [exchange(part, distance) for part, distance in zip(sent, distances)]
        if count == 1:
            following = {0: 1, 1: last}.get(stage)
            complete, some, held = single_level(first, following, held, arrays, complete)
        else:
            complete, some = local_level(first, count, arrays, complete)
        first += count
        kept.append(some)
        received, rows, complete, held = lax.optimization_barrier((received, rows, complete, held))
        if stage == 0:
            rows = jnp.concatenate([rows, received[0], received[1] + received[2]], 0)
        elif stage < 3:
            rows = jnp.concatenate([rows, *received], 0)
        if stage < 3:
            rows, complete, arrays = lax.optimization_barrier((rows, complete, arrays))
    spot = lax.axis_index("seq").astype(jnp.int32).reshape(1)
    return merge(spot, query, rows, received[0], kept, complete)


def solution(mesh):
    in_specs = (P("seq", None), P("seq", None), P("seq", None))
    out_specs = P("seq", None)
    return jax.shard_map(local, mesh=mesh, in_specs=in_specs, out_specs=out_specs, check_vma=False)
```

```python
import functools

import jax
import jax.numpy as jnp
from jax import lax
from jax.experimental import pallas as pl
from jax.experimental.pallas import tpu as pltpu
from jax.sharding import PartitionSpec as P

HEADS = 12
HEAD = 64
PAIR = 2 * HEAD
BLOCK = 512
TILE = 128
TILES = BLOCK // TILE
PAIRS = HEADS // 2
WIDTH = HEADS * HEAD
ROWS = 16
STRIDE = 256
UNIT = 2 * ROWS
PICK_VMEM = 50 << 20
LOCAL_VMEM = 52 << 20
MERGE_VMEM = 20 << 20
SINGLE_VMEM = 48 << 20

MASKED = -1e30
BF16 = jnp.bfloat16
F32 = jnp.float32
TRANSPOSED = (((1,), (1,)), ((), ()))

CHUNKS = (1, 1, 5, 1)
GROUPS = ((0, 3), (3, 5), (5, 6))


def owner_mask(rows, row_size, columns):
    row = lax.broadcasted_iota(jnp.int32, (rows, columns), 0) // row_size
    head = lax.broadcasted_iota(jnp.int32, (rows, columns), 1) // HEAD
    return row == head


def fetch_block(block, sources, targets, sems):
    rows = pl.ds(block * BLOCK, BLOCK)
    return [
        pltpu.make_async_copy(source.at[rows, :], target, sems.at[i])
        for i, (source, target) in enumerate(zip(sources, targets))
    ]


def pick_kernel(
    q_all, k_all, v_all, q_hbm, k_hbm, v_hbm, q_out, own_out, second_out, low_out, high_out, *refs
):
    targets, (q_ref, k_ref, v_ref), (corner_sems, block_sems) = refs[:3], refs[3:6], refs[6:]
    corners = [
        pltpu.make_async_copy(source.at[:, pl.ds(0, ROWS), :], target, corner_sems.at[i])
        for i, (source, target) in enumerate(
            ((q_all, q_ref), (k_all, k_ref), (v_all, v_ref))
        )
    ]
    blocks = fetch_block(0, (q_hbm, k_hbm, v_hbm), targets, block_sems)
    for copy in corners + blocks:
        copy.start()
    for copy in corners:
        copy.wait()
    owned = owner_mask(ROWS, 1, WIDTH)

    def diagonal(ref):
        return [
            jnp.sum(jnp.where(owned, ref[i].astype(F32), 0.0), axis=0, keepdims=True)
            for i in range(ROWS)
        ]

    def pack(rows):
        return jnp.concatenate(rows, 0).astype(BF16)

    q_out[...] = pack(diagonal(q_ref))
    for ref, columns in ((k_ref, slice(0, WIDTH)), (v_ref, slice(WIDTH, 2 * WIDTH))):
        rows = diagonal(ref)
        none = [jnp.zeros_like(rows[0])] * (ROWS // 4)
        own_out[:, columns] = pack(rows)
        second_out[:, columns] = pack(rows[::2])
        low_out[:, columns] = pack(rows[::4] + none)
        high_out[:, columns] = pack(none + rows[::4])
    for copy in blocks:
        copy.wait()


def pick(queries, key_rows, value_rows):
    arrays = (queries, key_rows, value_rows)
    shape = (ROWS, STRIDE, WIDTH)
    sizes = ((ROWS, WIDTH), (ROWS, 2 * WIDTH)) + ((ROWS // 2, 2 * WIDTH),) * 3
    sizes = sizes + ((BLOCK, WIDTH),) * 3
    return pl.pallas_call(
        pick_kernel,
        in_specs=[pl.BlockSpec(memory_space=pl.ANY)] * 6,
        out_specs=[pl.BlockSpec(memory_space=pltpu.VMEM)] * len(sizes),
        out_shape=[jax.ShapeDtypeStruct(size, BF16) for size in sizes],
        scratch_shapes=[pltpu.VMEM((ROWS, ROWS, WIDTH), BF16)] * 3
        + [pltpu.SemaphoreType.DMA((3,))] * 2,
        compiler_params=pltpu.CompilerParams(vmem_limit_bytes=PICK_VMEM),
        name="pick",
    )(*(array.reshape(shape) for array in arrays), *arrays)


def attend_block(q_ref, k_ref, v_ref, out_ref, kept_ref, after=lambda pair: None):
    low = lax.broadcasted_iota(jnp.int32, (1, PAIR), 1) < HEAD
    keep = lax.broadcasted_iota(
        jnp.int32, (TILE, 2 * TILE), 1
    ) % TILE <= lax.broadcasted_iota(jnp.int32, (TILE, 2 * TILE), 0)
    zero = jnp.zeros((TILE, PAIR), BF16)
    one = jnp.ones((TILE, PAIR), BF16)
    counters = jnp.where(low, one, zero), jnp.where(low, zero, one)

    def columns(pair):
        return slice(pair * PAIR, (pair + 1) * PAIR)

    def score(pair, j):
        query = q_ref[j * TILE :, columns(pair)] * jnp.asarray(HEAD**-0.5, BF16)
        key = k_ref[j * TILE : (j + 1) * TILE, columns(pair)]
        both = jnp.concatenate([jnp.where(low, key, zero), jnp.where(low, zero, key)], 0)
        return lax.dot_general(query, both, TRANSPOSED, preferred_element_type=F32)

    def soften(scores, t):
        parts = [scores[j][(t - j) * TILE : (t - j + 1) * TILE] for j in range(t + 1)]
        parts[t] = jnp.where(keep, parts[t], MASKED)
        most = parts[0]
        for part in parts[1:]:
            most = jnp.maximum(most, part)
        tops = [
            jnp.broadcast_to(
                jnp.max(most[:, start : start + TILE], axis=1, keepdims=True), (TILE, TILE)
            )
            for start in (0, TILE)
        ]
        top = jnp.concatenate(tops, 1)
        return jnp.concatenate([jnp.exp(part - top).astype(BF16) for part in parts], 1), tops

    def finish(pair, t, probs, tops):
        weights = []
        for j in range(t + 1):
            value = v_ref[j * TILE : (j + 1) * TILE, columns(pair)]
            weights.append(jnp.concatenate([jnp.where(low, value, zero), counters[0]], 1))
            weights.append(jnp.concatenate([jnp.where(low, zero, value), counters[1]], 1))
        both = jnp.dot(probs, jnp.concatenate(weights, 0), preferred_element_type=F32)
        upper, lower = both[:, :PAIR], both[:, PAIR:]
        out_ref[t * TILE : (t + 1) * TILE, columns(pair)] = (upper / lower).astype(BF16)
        if t * TILE % STRIDE == 0:
            a, b = 2 * pair, 2 * pair + 1
            for start, (x, y) in ((0, (upper, upper)), (2, (lower, lower)), (4, tops)):
                row = start + t * TILE // STRIDE
                kept_ref[row : row + 1, columns(pair)] = jnp.where(
                    low, x[a : a + 1], y[b : b + 1]
                )
        if t == TILES - 1:
            after(pair)

    ready = [score(0, j) for j in range(TILES)]
    waiting = []
    for pair in range(PAIRS):
        later = []
        for t in range(TILES):
            if pair + 1 < PAIRS:
                later.append(score(pair + 1, t))
            waiting.append((pair, t, *soften(ready, t)))
            if len(waiting) > 1:
                finish(*waiting.pop(0))
        ready = later
    finish(*waiting.pop(0))


def local_kernel(q_ref, k_ref, v_ref, *refs):
    attend_block(q_ref, k_ref, v_ref, *refs[-2:])


def single_kernel(first, following, q_ref, k_ref, v_ref, *refs):
    fetched = 0 if following is None else 3
    sources, refs = refs[:fetched], refs[-(5 + fetched) :]
    out_hbm, kept_ref, targets = refs[0], refs[1], refs[2 : 2 + fetched]
    out_ref, out_sems, block_sems = refs[2 + fetched :]
    blocks = fetch_block(following, sources, targets, block_sems) if fetched else []
    for copy in blocks:
        copy.start()

    def write(group):
        columns = pl.ds(group[0] * PAIR, (group[1] - group[0]) * PAIR)
        return pltpu.make_async_copy(
            out_ref.at[:, columns],
            out_hbm.at[pl.ds(first * BLOCK, BLOCK), columns],
            out_sems.at[GROUPS.index(group)],
        )

    def after(pair):
        for group in GROUPS:
            if group[1] == pair + 1:
                write(group).start()

    attend_block(q_ref, k_ref, v_ref, out_ref, kept_ref, after)
    for copy in [write(group) for group in GROUPS] + blocks:
        copy.wait()


def costs(count):
    return pl.CostEstimate(
        flops=count * HEADS * 4 * BLOCK * BLOCK * HEAD * 4,
        bytes_accessed=count * 8 * BLOCK * WIDTH,
        transcendentals=count * HEADS * BLOCK * BLOCK,
    )


def single_level(first, following, held, arrays, complete):
    anywhere = pl.BlockSpec(memory_space=pl.ANY)
    vmem = pl.BlockSpec(memory_space=pltpu.VMEM)
    operands = list(held)
    fetched = 0
    if following is not None:
        operands.extend(arrays)
        fetched = 3
    aliases = {}
    if complete is not None:
        aliases = {len(operands): 0}
        operands.append(complete)
    complete, kept, *held = pl.pallas_call(
        functools.partial(single_kernel, first, following),
        in_specs=[vmem] * 3 + [anywhere] * (len(operands) - 3),
        out_specs=[anywhere, vmem] + [vmem] * fetched,
        out_shape=[
            jax.ShapeDtypeStruct(arrays[0].shape, BF16),
            jax.ShapeDtypeStruct((8, WIDTH), F32),
        ]
        + [jax.ShapeDtypeStruct((BLOCK, WIDTH), BF16)] * fetched,
        input_output_aliases=aliases,
        scratch_shapes=[
            pltpu.VMEM((BLOCK, WIDTH), BF16),
            pltpu.SemaphoreType.DMA((len(GROUPS),)),
            pltpu.SemaphoreType.DMA((3,)),
        ],
        compiler_params=pltpu.CompilerParams(vmem_limit_bytes=SINGLE_VMEM),
        cost_estimate=costs(1),
        name="single",
    )(*operands)
    return complete, kept, held


def local_level(first, count, arrays, complete):
    spec = pl.BlockSpec((BLOCK, WIDTH), lambda i: (first + i, 0))
    operands = list(arrays)
    in_specs = [spec] * 3
    aliases = {}
    if complete is not None:
        operands.append(complete)
        in_specs.append(pl.BlockSpec(memory_space=pl.ANY))
        aliases = {3: 0}
    return pl.pallas_call(
        local_kernel,
        grid=(count,),
        in_specs=in_specs,
        out_specs=[spec, pl.BlockSpec((8, WIDTH), lambda i: (i, 0))],
        out_shape=[
            jax.ShapeDtypeStruct(arrays[0].shape, BF16),
            jax.ShapeDtypeStruct((8 * count, WIDTH), F32),
        ],
        input_output_aliases=aliases,
        compiler_params=pltpu.CompilerParams(vmem_limit_bytes=LOCAL_VMEM),
        cost_estimate=costs(count),
        name="local",
    )(*operands)


def merge_kernel(spot_ref, q_ref, own_ref, other_ref, *refs):
    kept_refs, old_ref, out_ref, corner, sems = refs[:-5], refs[-5], refs[-4], refs[-3], refs[-2:]
    old = pltpu.make_async_copy(old_ref.at[:, pl.ds(0, ROWS), :], corner, sems[0])
    old.start()
    lanes = HEADS * ROWS
    owned = owner_mask(lanes, ROWS, WIDTH)
    query = q_ref[...] * jnp.asarray(HEAD**-0.5, BF16)
    spread = jnp.where(owned, jnp.concatenate([query] * HEADS, 0), jnp.zeros((), BF16))
    score = jnp.concatenate(
        [
            lax.dot_general(spread, ref[:, :WIDTH], TRANSPOSED, preferred_element_type=F32)
            for ref in (own_ref, other_ref)
        ],
        1,
    )
    keys = score.shape[1]
    device = spot_ref[0]
    column = lax.broadcasted_iota(jnp.int32, (1, keys), 1)
    core, x, z = column // (keys // 2), column // (4 * UNIT) % 4, column // UNIT % 4
    inner = column % UNIT
    quarter = jnp.where(inner < 16, 0, jnp.where(inner < 24, 1, jnp.where(inner < 28, 2, 3)))
    index = jnp.where(
        inner < 16, inner, jnp.where(inner < 24, 2 * (inner - 16), 4 * (inner % 4))
    )
    source = jnp.bitwise_xor(device, quarter * 32 + x * 8 + z * 2 + core)
    key_place = source * ROWS + index
    row = lax.broadcasted_iota(jnp.int32, (lanes, 1), 0) % ROWS
    query_place = device * ROWS + row
    in_one = (quarter == 0).astype(F32)
    in_two = jnp.where((quarter <= 1) & (index % 2 == 0), 1.0, 0.0)
    in_three = jnp.where(index % 4 == 0, 1.0, 0.0)
    has_two = jnp.where(row % 2 == 0, 1.0, 0.0)
    has_three = jnp.where(row % 4 == 0, 1.0, 0.0)
    count = in_one + has_two * in_two + has_three * in_three
    count = jnp.where(key_place <= query_place, count, 0.0)
    score = jnp.where(count > 0.0, score, MASKED)
    top = jnp.max(score, axis=1, keepdims=True)
    probs = jnp.exp(score - top) * count
    total = jnp.sum(probs, axis=1, keepdims=True)
    probs = probs.astype(BF16)
    result = jnp.dot(probs[:, : keys // 2], own_ref[:, WIDTH:], preferred_element_type=F32)
    result = result + jnp.dot(
        probs[:, keys // 2 :], other_ref[:, WIDTH:], preferred_element_type=F32
    )

    def gather_heads(array):
        kept = jnp.where(owned, array, 0.0)
        return jnp.sum(kept.reshape(HEADS, ROWS, WIDTH), axis=0)

    top, total, result = gather_heads(top), gather_heads(total), gather_heads(result)
    blocks = [ref[8 * i : 8 * i + 8] for ref in kept_refs for i in range(ref.shape[0] // 8)]
    result_zero, total_zero, top_zero = (
        jnp.concatenate([block[start : start + 2] for block in blocks], 0) for start in (0, 2, 4)
    )
    best = jnp.maximum(top, top_zero)
    weight, weight_zero = jnp.exp(top - best), jnp.exp(top_zero - best)
    mixed = (weight * result + weight_zero * result_zero) / (
        weight * total + weight_zero * total_zero
    )
    owned = owner_mask(ROWS, 1, WIDTH)
    old.wait()
    for i in range(ROWS):
        corner[i] = jnp.where(owned, mixed[i : i + 1], corner[i].astype(F32)).astype(BF16)
    new = pltpu.make_async_copy(corner, out_ref.at[:, pl.ds(0, ROWS), :], sems[1])
    new.start()
    new.wait()


def merge(spot, query, own, other, kept, complete):
    shape = (ROWS, STRIDE, WIDTH)
    held = pl.BlockSpec(memory_space=pltpu.VMEM)
    anywhere = pl.BlockSpec(memory_space=pl.ANY)
    merged = pl.pallas_call(
        merge_kernel,
        in_specs=[pl.BlockSpec(memory_space=pltpu.SMEM)] + [held] * (3 + len(kept)) + [anywhere],
        out_specs=anywhere,
        out_shape=jax.ShapeDtypeStruct(shape, BF16),
        input_output_aliases={4 + len(kept): 0},
        scratch_shapes=[
            pltpu.VMEM((ROWS, ROWS, WIDTH), BF16),
            pltpu.SemaphoreType.DMA,
            pltpu.SemaphoreType.DMA,
        ],
        compiler_params=pltpu.CompilerParams(vmem_limit_bytes=MERGE_VMEM),
        name="merge",
    )(spot, query, own, other, *kept, complete.reshape(shape))
    return merged.reshape(complete.shape)


def local(queries, key_rows, value_rows):
    devices = lax.axis_size("seq")
    arrays = (queries, key_rows, value_rows)

    def exchange(array, distance):
        return lax.ppermute(array, "seq", [(i, i ^ distance) for i in range(devices)])

    query, rows, near, low, high, *held = pick(*arrays)
    sent = [near, low, high]
    complete, kept, first = None, [], 0
    stages = ((32, 64, 96), (2, 4, 6), (8, 16, 24), (1,))
    for stage, (distances, count) in enumerate(zip(stages, CHUNKS)):
        if stage > 0:
            sent = [rows] * len(distances)
        received = [exchange(part, distance) for part, distance in zip(sent, distances)]
        if stage < 2:
            following = 1 if stage == 0 else None
            complete, some, held = single_level(first, following, held, arrays, complete)
        else:
            complete, some = local_level(first, count, arrays, complete)
        first += count
        kept.append(some)
        received, rows, complete, held = lax.optimization_barrier((received, rows, complete, held))
        if stage == 0:
            rows = jnp.concatenate([rows, received[0], received[1] + received[2]], 0)
        elif stage < 3:
            rows = jnp.concatenate([rows, *received], 0)
        if stage < 3:
            rows, complete, arrays = lax.optimization_barrier((rows, complete, arrays))
    spot = lax.axis_index("seq").astype(jnp.int32).reshape(1)
    return merge(spot, query, rows, received[0], kept, complete)


def solution(mesh):
    in_specs = (P("seq", None), P("seq", None), P("seq", None))
    out_specs = P("seq", None)
    return jax.shard_map(local, mesh=mesh, in_specs=in_specs, out_specs=out_specs, check_vma=False)
```
